32 devices in a mesh: section: 2 (over core), task: 4 (over y, x), fsdp: 4 (over z).
Axes of the slice: x: 2, y: 2, z: 4, core: 2. Of those that a mesh axis runs over, the one named last changes fastest.
Arguments:
- states: bfloat16 [4, 192, 2048], P('task', 'fsdp'), may hold values from -6 to 6
- task_weights: bfloat16 [4, 2, 2, 2048, 5120], P('task', 'section', None, None, 'fsdp'), may hold values from -0.125 to 0.125
- pad_mask: int32 [4, 192], P('task', 'fsdp'), may hold values 0 or 1
- direction: float32 [2, 2048, 2, 5120], P('section', ('task', 'fsdp')), may hold values from -0.125 to 0.125
- residual: float32 [2, 2048, 2, 5120], P('section', ('task', 'fsdp')), may hold values from -6 to 6
Outputs:
- residual_next: float32 [2, 2048, 2, 5120], P('section', ('task', 'fsdp'))
- direction_next: float32 [2, 2048, 2, 5120], P('section', ('task', 'fsdp'))
- step_size: float32 [], replicated
The draws below stay inside these ranges and needn't reach their ends.
All inputs are finite; a program needn't handle non-finite values. No bound on the sum of `pad_mask` on one device may be relied on, other than what follows from the above.
Results may differ from the reference program's by a relative error of at most 0.0052.
Values may be sent and summed in bfloat16 or wider, within the bound.
No kernel may reach another device: no remote copies, remote signals or barrier semaphores. Data moves between devices by JAX's collectives and lax.ppermute only.
A program may use at most 192 MiB of HBM per device.

```python
import jax
import jax.numpy as jnp
from jax import lax

D = 2048
FF = 5120
TOKENS = 192
LAYERS = 2
TASKS = 4


def touch_ends(array, rng, low, top_value):
    longest = array.shape.index(max(array.shape))
    spots = []
    for shift in (0, 1):
        where = [jax.random.randint(jax.random.fold_in(rng, axis), (), 0, length) for axis, length in enumerate(array.shape)]
        where[longest] = (where[longest] + shift) % array.shape[longest]
        spots.append(tuple(where))
    return array.at[spots[0]].set(low).at[spots[1]].set(top_value)


def steps_of(key, shape, pieces, smallest, top_value):
    level, own = 1.0, jax.random.fold_in(key, 6)
    for axis_at, shards_of in pieces:
        draws = jnp.exp(jax.random.uniform(jax.random.fold_in(own, axis_at), (shards_of,), jnp.float32, smallest / len(pieces), top_value / len(pieces)))
        level = level * jnp.repeat(draws, shape[axis_at] // shards_of).reshape([-1 if axis == axis_at else 1 for axis in range(len(shape))])
    return level


def centred(own_key, shape, scale, limit, cuts=(), held_as=jnp.bfloat16):
    array = jax.random.normal(own_key, shape, jnp.float32) * scale
    if len(cuts) > 0:
        array = steps_of(own_key, shape, cuts, -0.22, 0.18) * array
    return jnp.clip(array, min=-limit, max=limit).astype(held_as)


def setup_inputs(seed: int = 0) -> dict:
    streams_of = jax.random.split(jax.random.key(seed), 6)
    states = centred(streams_of[0], (TASKS, TOKENS, D), 1.0, 6.0, ((0, 4), (1, 4)))
    task_weights = centred(streams_of[1], (TASKS, LAYERS, 2, D, FF), D ** -0.5, 0.125, ((0, 4), (1, 2), (4, 4)))
    pad_mask = touch_ends((jax.random.randint(streams_of[2], (TASKS, TOKENS), 0, 4) < 3).astype(jnp.int32), jax.random.fold_in(streams_of[2], 1), 0, 1)
    direction = centred(streams_of[3], (LAYERS, D, 2, FF), D ** -0.5, 0.125, ((0, 2), (1, 16)), jnp.float32)
    residual = centred(streams_of[4], (LAYERS, D, 2, FF), 1.0, 6.0, ((0, 2), (1, 16)), jnp.float32)
    return {"states": states, "task_weights": task_weights, "pad_mask": pad_mask, "direction": direction, "residual": residual}


eps_norm = 1e-06

def normalize(token_rows):
    return token_rows * lax.rsqrt(lax.optimization_barrier(jnp.mean(token_rows * token_rows, axis=-1, keepdims=True)) + eps_norm)

def gelu_tanh(values):
    return jax.nn.gelu(values, approximate=True)

def across_hidden(left_side, right_side):
    return lax.dot_general(left_side, right_side, (((1,), (1,)), ((), ())), preferred_element_type=jnp.float32)

def across_tokens(left_side, right_side):
    return lax.dot_general(left_side, right_side, (((0,), (0,)), ((), ())), preferred_element_type=jnp.float32)

def task_product(token_rows, weights, keep_mask, steering):
    current = token_rows
    current_dot = jnp.zeros_like(token_rows)
    saved_acts = []
    for layer_idx in range(LAYERS):
        w_in = weights[layer_idx, 0]
        w_out = weights[layer_idx, 1]
        steer_in = steering[layer_idx, :, 0, :]
        steer_out = steering[layer_idx, :, 1, :]
        widened = current.astype(jnp.float32)
        widened_dot = current_dot.astype(jnp.float32)
        normed, normed_dot = jax.jvp(normalize, (widened,), (widened_dot,))
        normed_b = normed.astype(jnp.bfloat16)
        normed_dot_b = normed_dot.astype(jnp.bfloat16)
        preact = jnp.dot(normed_b, w_in, preferred_element_type=jnp.float32)
        preact_dot = jnp.dot(normed_dot_b, w_in, preferred_element_type=jnp.float32) + jnp.dot(normed_b, steer_in, preferred_element_type=jnp.float32)
        hidden, slope_vals = jax.jvp(gelu_tanh, (preact,), (jnp.ones_like(preact),))
        hidden_b = hidden.astype(jnp.bfloat16)
        hidden_dot_b = (slope_vals * preact_dot).astype(jnp.bfloat16)
        mixed_out = across_hidden(hidden_b, w_out)
        mixed_dot = across_hidden(hidden_dot_b, w_out) + across_hidden(hidden_b, steer_out)
        saved_acts.append((widened, normed_b, hidden_b, slope_vals))
        current = (widened + mixed_out).astype(jnp.bfloat16)
        current_dot = (widened_dot + mixed_dot).astype(jnp.bfloat16)
    cotangent = current_dot * keep_mask[:, None].astype(jnp.bfloat16)
    layer_terms = [None] * LAYERS
    for layer_idx in reversed(range(LAYERS)):
        widened, normed_b, hidden_b, slope_vals = saved_acts[layer_idx]
        w_in = weights[layer_idx, 0]
        w_out = weights[layer_idx, 1]
        hidden_bar = jnp.dot(cotangent, w_out, preferred_element_type=jnp.float32)
        preact_bar = (hidden_bar * slope_vals).astype(jnp.bfloat16)
        normed_bar = across_hidden(preact_bar, w_in)
        layer_terms[layer_idx] = jnp.stack([across_tokens(normed_b, preact_bar), across_tokens(cotangent, hidden_b)], axis=1)
        pullback = jax.vjp(normalize, widened)[1]
        cotangent = (cotangent.astype(jnp.float32) + pullback(normed_bar)[0]).astype(jnp.bfloat16)
    return jnp.stack(layer_terms)

def reference(states, task_weights, pad_mask, direction, residual):
    steering = direction.astype(jnp.bfloat16)
    curvature_sum = jnp.zeros(direction.shape, jnp.float32)
    for task_idx in range(TASKS):
        curvature_sum = curvature_sum + task_product(states[task_idx], task_weights[task_idx], pad_mask[task_idx], steering)
    start_norm = jnp.sum(residual * residual)
    curvature = jnp.sum(direction * curvature_sum)
    step_size = start_norm / curvature
    residual_next = residual - step_size * curvature_sum
    next_norm = jnp.sum(residual_next * residual_next)
    direction_next = residual_next + next_norm / start_norm * direction
    return (residual_next, direction_next, step_size)
```

```python
import jax
import jax.numpy as jnp
from jax import lax
from jax.sharding import PartitionSpec as P

ALL = ("section", "task", "fsdp")
eps_norm = 1e-06


def normalize(token_rows):
    return token_rows * lax.rsqrt(
        jnp.mean(token_rows * token_rows, axis=-1, keepdims=True) + eps_norm
    )


def gelu_tanh(values):
    return jax.nn.gelu(values, approximate=True)


def across_hidden(left_side, right_side):
    return lax.dot_general(
        left_side, right_side, (((1,), (1,)), ((), ())), preferred_element_type=jnp.float32
    )


def across_tokens(left_side, right_side):
    return lax.dot_general(
        left_side, right_side, (((0,), (0,)), ((), ())), preferred_element_type=jnp.float32
    )


def dot(left_side, right_side):
    return jnp.dot(left_side, right_side, preferred_element_type=jnp.float32)


def send(value, route):
    sections, tasks, shards = (lax.axis_size(axis) for axis in ALL)
    pairs = []
    for s in range(sections):
        for t in range(tasks):
            for f in range(shards):
                target = route(s, t, f)
                if target is not None:
                    to_s, to_t, to_f = target
                    pairs.append(
                        ((s * tasks + t) * shards + f, (to_s * tasks + to_t) * shards + to_f)
                    )
    return lax.ppermute(value, ALL, pairs)


def between(start, end, k):
    return lambda s, t, f: (end, t, f ^ k) if s == start else None


def gather_rows(rows, start, end):
    parts = []
    for k in range(lax.axis_size("fsdp")):
        if k == 0 and start == end:
            parts.append(rows)
        else:
            parts.append(send(rows, between(start, end, k)))
    return jnp.concatenate(parts, axis=0)


def scatter_sum(partial, start, end):
    shards = lax.axis_size("fsdp")
    blocks = partial.reshape(shards, partial.shape[0] // shards, partial.shape[1])
    total = None
    for k in range(shards):
        if k == 0 and start == end:
            part = blocks[0]
        else:
            part = send(blocks[k].astype(jnp.bfloat16), between(start, end, k)).astype(jnp.float32)
        total = part if total is None else total + part
    return total


def task_partners(value_of):
    parts = [value_of(0)]
    for k in range(1, lax.axis_size("task")):
        parts.append(send(value_of(k), lambda s, t, f, k=k: (s, t ^ k, f)))
    return parts


def fsdp_partners(value_of):
    parts = [value_of(0)]
    for k in range(1, lax.axis_size("fsdp")):
        parts.append(send(value_of(k), lambda s, t, f, k=k: (s, t, f ^ k)))
    return parts


def in_order(parts, index, axis):
    stacked = jnp.stack(parts)
    return jnp.concatenate(
        [
            lax.dynamic_index_in_dim(stacked, index ^ j, 0, keepdims=False)
            for j in range(len(parts))
        ],
        axis=axis,
    )


def sum_everywhere(value):
    for axis in ALL:
        count = lax.axis_size(axis)
        parts = [value]
        for k in range(1, count):
            parts.append(lax.ppermute(value, axis, [(i, i ^ k) for i in range(count)]))
        while len(parts) > 1:
            parts = [parts[i] + parts[i + 1] for i in range(0, len(parts), 2)]
        value = parts[0]
    return value


def on_device(states, task_weights, pad_mask, direction, residual):
    sections = lax.axis_size("section")
    tasks = lax.axis_size("task")
    shards = lax.axis_size("fsdp")
    section_id = lax.axis_index("section")
    task_id = lax.axis_index("task")
    shard_id = lax.axis_index("fsdp")
    w_in = task_weights[0, 0, 0]
    w_out = task_weights[0, 0, 1]
    width, hidden = w_in.shape
    row_count = states.shape[1]
    joined = row_count * shards
    block = width // tasks
    piece = block // shards
    direc_local = direction[0]
    resid_local = residual[0]

    narrow = [direc_local[:, i, :].astype(jnp.bfloat16) for i in range(2)]

    def direction_for(k):
        at = (shard_id ^ k) * hidden
        return jnp.stack([lax.dynamic_slice_in_dim(part, at, hidden, 1) for part in narrow])

    steering = in_order(fsdp_partners(direction_for), shard_id, 1)
    steer_in, steer_out = steering[0], steering[1]

    own_rows = states[0]
    rows_all = gather_rows(own_rows, 0, 0)
    for layer in range(sections):
        normed = normalize(rows_all.astype(jnp.float32))
        normed_b = normed.astype(jnp.bfloat16)
        preact = dot(normed_b, w_in)
        acted, slope = jax.jvp(gelu_tanh, (preact,), (jnp.ones_like(preact),))
        acted_b = acted.astype(jnp.bfloat16)
        if layer + 1 < sections:
            mixed = scatter_sum(across_hidden(acted_b, w_out), layer, layer)
            after = (own_rows.astype(jnp.float32) + mixed).astype(jnp.bfloat16)
            arrived = gather_rows(after, layer, layer + 1)
            here = section_id == layer + 1
            rows_all = jnp.where(here, arrived, rows_all)
            own_rows = jnp.where(here, arrived[:row_count], own_rows)

    def features_for(array):
        return lambda k: lax.dynamic_slice_in_dim(array, (task_id ^ k) * block, block, 1)

    normed_tasks = jnp.concatenate(task_partners(features_for(normed_b)), axis=0)
    acted_tasks = jnp.concatenate(task_partners(lambda k: acted_b), axis=0)
    steered_parts = dot(normed_tasks, steer_in).reshape(tasks, joined, hidden)
    steered = task_partners(
        lambda k: steered_parts[k] if k == 0 else steered_parts[k].astype(jnp.bfloat16)
    )
    steered = sum(part.astype(jnp.float32) for part in steered)
    turned_parts = across_hidden(acted_tasks, steer_out).astype(jnp.bfloat16)
    turned_parts = turned_parts.reshape(tasks, joined, block)
    turned = in_order(task_partners(lambda k: turned_parts[k]), task_id, 1).astype(jnp.float32)

    own_dot = jnp.zeros((row_count, width), jnp.bfloat16)
    for layer in range(sections):
        if layer == 0:
            preact_dot = steered
        else:
            normed_dot = jax.jvp(
                normalize, (rows_all.astype(jnp.float32),), (dots_all.astype(jnp.float32),)
            )[1]
            preact_dot = dot(normed_dot.astype(jnp.bfloat16), w_in) + steered
        acted_dot_b = (slope * preact_dot).astype(jnp.bfloat16)
        mixed_dot = scatter_sum(across_hidden(acted_dot_b, w_out) + turned, layer, layer)
        after_dot = (own_dot.astype(jnp.float32) + mixed_dot).astype(jnp.bfloat16)
        if layer + 1 < sections:
            dots_all = gather_rows(after_dot, layer, layer + 1)
            own_dot = dots_all[:row_count]

    own_bar = after_dot * pad_mask[0][:, None].astype(jnp.bfloat16)
    for layer in reversed(range(sections)):
        if layer == sections - 1:
            bars_all = gather_rows(own_bar, layer, layer)
        else:
            arrived = gather_rows(own_bar, layer + 1, layer)
            here = section_id == layer
            bars_all = jnp.where(here, arrived, bars_all)
            own_bar = jnp.where(here, arrived[:row_count], own_bar)
        preact_bar = (dot(bars_all, w_out) * slope).astype(jnp.bfloat16)
        if layer > 0:
            normed_bar = scatter_sum(across_hidden(preact_bar, w_in), layer, layer)
            pullback = jax.vjp(normalize, own_rows.astype(jnp.float32))[1]
            own_bar = (own_bar.astype(jnp.float32) + pullback(normed_bar)[0]).astype(jnp.bfloat16)

    bars_tasks = jnp.concatenate(task_partners(features_for(bars_all)), axis=0)
    preact_bars_tasks = jnp.concatenate(task_partners(lambda k: preact_bar), axis=0)
    curved = [
        across_tokens(normed_tasks, preact_bars_tasks).astype(jnp.bfloat16),
        across_tokens(bars_tasks, acted_tasks).astype(jnp.bfloat16),
    ]

    def curved_for(k):
        at = (shard_id ^ k) * piece
        return jnp.stack([lax.dynamic_slice_in_dim(part, at, piece, 0) for part in curved])

    product = in_order(fsdp_partners(curved_for), shard_id, 2).astype(jnp.float32)
    product = jnp.transpose(product, (1, 0, 2))

    sums = sum_everywhere(
        jnp.stack(
            [
                jnp.sum(resid_local * resid_local),
                jnp.sum(direc_local * product),
                jnp.sum(resid_local * product),
                jnp.sum(product * product),
            ]
        )
    )
    start_norm, curvature, crossed, squared = sums[0], sums[1], sums[2], sums[3]
    step_size = start_norm / curvature
    next_norm = start_norm - 2.0 * step_size * crossed + step_size * step_size * squared
    resid_next = resid_local - step_size * product
    direc_next = resid_next + next_norm / start_norm * direc_local
    return (resid_next[None], direc_next[None], step_size)


def solution(mesh):
    placed = (
        P("task", "fsdp", None),
        P("task", "section", None, None, "fsdp"),
        P("task", "fsdp"),
        P("section", ("task", "fsdp"), None, None),
        P("section", ("task", "fsdp"), None, None),
    )
    return jax.shard_map(
        on_device,
        mesh=mesh,
        in_specs=placed,
        out_specs=(
            P("section", ("task", "fsdp"), None, None),
            P("section", ("task", "fsdp"), None, None),
            P(),
        ),
        check_vma=False,
    )
```

```python
import jax
import jax.numpy as jnp
from jax import lax
from jax.sharding import PartitionSpec as P

ALL = ("section", "task", "fsdp")
eps_norm = 1e-06


def normalize(token_rows):
    return token_rows * lax.rsqrt(
        jnp.mean(token_rows * token_rows, axis=-1, keepdims=True) + eps_norm
    )


def gelu_tanh(values):
    return jax.nn.gelu(values, approximate=True)


def across_hidden(left_side, right_side):
    return lax.dot_general(
        left_side, right_side, (((1,), (1,)), ((), ())), preferred_element_type=jnp.float32
    )


def across_tokens(left_side, right_side):
    return lax.dot_general(
        left_side, right_side, (((0,), (0,)), ((), ())), preferred_element_type=jnp.float32
    )


def dot(left_side, right_side):
    return jnp.dot(left_side, right_side, preferred_element_type=jnp.float32)


def send(value, route):
    sections, tasks, shards = (lax.axis_size(axis) for axis in ALL)
    pairs = []
    for s in range(sections):
        for t in range(tasks):
            for f in range(shards):
                target = route(s, t, f)
                if target is not None:
                    to_s, to_t, to_f = target
                    pairs.append(
                        ((s * tasks + t) * shards + f, (to_s * tasks + to_t) * shards + to_f)
                    )
    return lax.ppermute(value, ALL, pairs)


def between(start, end, k):
    return lambda s, t, f: (end, t, f ^ k) if s == start else None


def gather_rows(rows, start, end):
    parts = []
    for k in range(lax.axis_size("fsdp")):
        if k == 0 and start == end:
            parts.append(rows)
        else:
            parts.append(send(rows, between(start, end, k)))
    return jnp.concatenate(parts, axis=0)


def scatter_sum(partial, start, end):
    shards = lax.axis_size("fsdp")
    blocks = partial.reshape(shards, partial.shape[0] // shards, partial.shape[1])
    total = None
    for k in range(shards):
        if k == 0 and start == end:
            part = blocks[0]
        else:
            part = send(blocks[k].astype(jnp.bfloat16), between(start, end, k)).astype(jnp.float32)
        total = part if total is None else total + part
    return total


def task_partners(value_of):
    parts = [value_of(0)]
    for k in range(1, lax.axis_size("task")):
        parts.append(send(value_of(k), lambda s, t, f, k=k: (s, t ^ k, f)))
    return parts


def fsdp_partners(value_of):
    parts = [value_of(0)]
    for k in range(1, lax.axis_size("fsdp")):
        parts.append(send(value_of(k), lambda s, t, f, k=k: (s, t, f ^ k)))
    return parts


def tie(value, other):
    return lax.optimization_barrier((value, other))


def in_order(parts, index, axis):
    stacked = jnp.stack(parts)
    return jnp.concatenate(
        [
            lax.dynamic_index_in_dim(stacked, index ^ j, 0, keepdims=False)
            for j in range(len(parts))
        ],
        axis=axis,
    )


def sum_everywhere(value):
    for axis in ALL:
        count = lax.axis_size(axis)
        parts = [value]
        for k in range(1, count):
            parts.append(lax.ppermute(value, axis, [(i, i ^ k) for i in range(count)]))
        while len(parts) > 1:
            parts = [parts[i] + parts[i + 1] for i in range(0, len(parts), 2)]
        value = parts[0]
    return value


def on_device(states, task_weights, pad_mask, direction, residual):
    sections = lax.axis_size("section")
    tasks = lax.axis_size("task")
    shards = lax.axis_size("fsdp")
    section_id = lax.axis_index("section")
    task_id = lax.axis_index("task")
    shard_id = lax.axis_index("fsdp")
    w_in = task_weights[0, 0, 0]
    w_out = task_weights[0, 0, 1]
    width, hidden = w_in.shape
    row_count = states.shape[1]
    joined = row_count * shards
    block = width // tasks
    piece = block // shards
    direc_local = direction[0]
    resid_local = residual[0]

    narrow = [direc_local[:, i, :].astype(jnp.bfloat16) for i in range(2)]

    def direction_for(k):
        at = (shard_id ^ k) * hidden
        return jnp.stack([lax.dynamic_slice_in_dim(part, at, hidden, 1) for part in narrow])

    pieces = fsdp_partners(direction_for)

    own_inputs = [states[0]]
    rows_all = gather_rows(states[0], 0, 0)
    for layer in range(sections):
        normed = normalize(rows_all.astype(jnp.float32))
        normed_b = normed.astype(jnp.bfloat16)
        preact = dot(normed_b, w_in)
        acted, slope = jax.jvp(gelu_tanh, (preact,), (jnp.ones_like(preact),))
        acted_b = acted.astype(jnp.bfloat16)
        if layer + 1 < sections:
            mixed = across_hidden(acted_b, w_out)
            if layer == 0:
                mixed, pieces[1] = tie(mixed, pieces[1])
            mixed = scatter_sum(mixed, layer, 0)
            own_rows = (own_inputs[layer].astype(jnp.float32) + mixed).astype(jnp.bfloat16)
            if layer == 0:
                own_rows, pieces[2] = tie(own_rows, pieces[2])
            own_inputs.append(own_rows)
            arrived = gather_rows(own_rows, 0, layer + 1)
            rows_all = jnp.where(section_id == layer + 1, arrived, rows_all)

    steering = in_order(pieces, shard_id, 1)
    steer_in, steer_out = steering[0], steering[1]

    def features_for(array):
        return lambda k: lax.dynamic_slice_in_dim(array, (task_id ^ k) * block, block, 1)

    normed_tasks = jnp.concatenate(task_partners(features_for(normed_b)), axis=0)
    acted_tasks = jnp.concatenate(task_partners(lambda k: acted_b), axis=0)
    steered_parts = dot(normed_tasks, steer_in).reshape(tasks, joined, hidden)
    steered = task_partners(
        lambda k: steered_parts[k] if k == 0 else steered_parts[k].astype(jnp.bfloat16)
    )
    steered = sum(part.astype(jnp.float32) for part in steered)
    turned_parts = across_hidden(acted_tasks, steer_out).astype(jnp.bfloat16)
    turned_parts = turned_parts.reshape(tasks, joined, block)
    turned = in_order(task_partners(lambda k: turned_parts[k]), task_id, 1).astype(jnp.float32)

    own_dot = jnp.zeros((row_count, width), jnp.bfloat16)
    for layer in range(sections):
        if layer == 0:
            preact_dot = steered
        else:
            dots_all = gather_rows(own_dot, 0, layer)
            normed_dot = jax.jvp(
                normalize, (rows_all.astype(jnp.float32),), (dots_all.astype(jnp.float32),)
            )[1]
            preact_dot = dot(normed_dot.astype(jnp.bfloat16), w_in) + steered
        acted_dot_b = (slope * preact_dot).astype(jnp.bfloat16)
        mixed_dot = scatter_sum(across_hidden(acted_dot_b, w_out) + turned, layer, 0)
        own_dot = (own_dot.astype(jnp.float32) + mixed_dot).astype(jnp.bfloat16)

    own_bar = own_dot * pad_mask[0][:, None].astype(jnp.bfloat16)
    bars_all = jnp.zeros((joined, width), jnp.bfloat16)
    for layer in reversed(range(sections)):
        arrived = gather_rows(own_bar, 0, layer)
        bars_all = jnp.where(section_id == layer, arrived, bars_all)
        preact_bar = (dot(bars_all, w_out) * slope).astype(jnp.bfloat16)
        if layer > 0:
            normed_bar = scatter_sum(across_hidden(preact_bar, w_in), layer, 0)
            pullback = jax.vjp(normalize, own_inputs[layer].astype(jnp.float32))[1]
            own_bar = (own_bar.astype(jnp.float32) + pullback(normed_bar)[0]).astype(jnp.bfloat16)

    def to_owners(curved):
        curved = curved.astype(jnp.bfloat16).reshape(shards, piece, hidden)

        def curved_for(k):
            return lax.dynamic_index_in_dim(curved, shard_id ^ k, 0, keepdims=False)

        return in_order(fsdp_partners(curved_for), shard_id, 1)

    bars_tasks = jnp.concatenate(task_partners(features_for(bars_all)), axis=0)
    curved_out = to_owners(across_tokens(bars_tasks, acted_tasks))
    preact_bars_tasks = jnp.concatenate(task_partners(lambda k: preact_bar), axis=0)
    curved_in = to_owners(across_tokens(normed_tasks, preact_bars_tasks))
    product = jnp.stack([curved_in, curved_out], axis=1).astype(jnp.float32)

    sums = sum_everywhere(
        jnp.stack(
            [
                jnp.sum(resid_local * resid_local),
                jnp.sum(direc_local * product),
                jnp.sum(resid_local * product),
                jnp.sum(product * product),
            ]
        )
    )
    start_norm, curvature, crossed, squared = sums[0], sums[1], sums[2], sums[3]
    step_size = start_norm / curvature
    next_norm = start_norm - 2.0 * step_size * crossed + step_size * step_size * squared
    resid_next = resid_local - step_size * product
    direc_next = resid_next + next_norm / start_norm * direc_local
    return (resid_next[None], direc_next[None], step_size)


def solution(mesh):
    placed = (
        P("task", "fsdp", None),
        P("task", "section", None, None, "fsdp"),
        P("task", "fsdp"),
        P("section", ("task", "fsdp"), None, None),
        P("section", ("task", "fsdp"), None, None),
    )
    return jax.shard_map(
        on_device,
        mesh=mesh,
        in_specs=placed,
        out_specs=(
            P("section", ("task", "fsdp"), None, None),
            P("section", ("task", "fsdp"), None, None),
            P(),
        ),
        check_vma=False,
    )
```

```python
import jax
import jax.numpy as jnp
from jax import lax
from jax.experimental import pallas as pl
from jax.experimental.pallas import tpu as pltpu
from jax.experimental.layout import Layout, with_layout_constraint
from jax.sharding import PartitionSpec as P

ALL = ("section", "task", "fsdp")
eps_norm = 1e-06


def normalize(token_rows):
    return token_rows * lax.rsqrt(
        jnp.mean(token_rows * token_rows, axis=-1, keepdims=True) + eps_norm
    )


def gelu_tanh(values):
    return jax.nn.gelu(values, approximate=True)


def across_hidden(left_side, right_side):
    return lax.dot_general(
        left_side, right_side, (((1,), (1,)), ((), ())), preferred_element_type=jnp.float32
    )


def across_tokens(left_side, right_side):
    return lax.dot_general(
        left_side, right_side, (((0,), (0,)), ((), ())), preferred_element_type=jnp.float32
    )


def dot(left_side, right_side):
    return jnp.dot(left_side, right_side, preferred_element_type=jnp.float32)


def send(value, route):
    sections, tasks, shards = (lax.axis_size(axis) for axis in ALL)
    pairs = []
    for s in range(sections):
        for t in range(tasks):
            for f in range(shards):
                target = route(s, t, f)
                if target is not None:
                    to_s, to_t, to_f = target
                    pairs.append(
                        ((s * tasks + t) * shards + f, (to_s * tasks + to_t) * shards + to_f)
                    )
    return lax.ppermute(value, ALL, pairs)


def between(start, end, k):
    return lambda s, t, f: (end, t, f ^ k) if s == start else None


def gather_rows(rows, start, end):
    parts = []
    for k in range(lax.axis_size("fsdp")):
        if k == 0 and start == end:
            parts.append(rows)
        else:
            parts.append(send(rows, between(start, end, k)))
    return jnp.concatenate(parts, axis=0)


def scatter_sum(partial, start, end):
    shards = lax.axis_size("fsdp")
    blocks = partial.reshape(shards, partial.shape[0] // shards, partial.shape[1])
    total = None
    for k in range(shards):
        if k == 0 and start == end:
            part = blocks[0]
        else:
            part = send(blocks[k].astype(jnp.bfloat16), between(start, end, k)).astype(jnp.float32)
        total = part if total is None else total + part
    return total


def task_partners(value_of):
    parts = [value_of(0)]
    for k in range(1, lax.axis_size("task")):
        parts.append(send(value_of(k), lambda s, t, f, k=k: (s, t ^ k, f)))
    return parts


def fsdp_partners(value_of):
    parts = [value_of(0)]
    for k in range(1, lax.axis_size("fsdp")):
        parts.append(send(value_of(k), lambda s, t, f, k=k: (s, t, f ^ k)))
    return parts


def tie(value, other):
    return lax.optimization_barrier((value, other))


def in_order(parts, index, axis):
    stacked = jnp.stack(parts)
    return jnp.concatenate(
        [
            lax.dynamic_index_in_dim(stacked, index ^ j, 0, keepdims=False)
            for j in range(len(parts))
        ],
        axis=axis,
    )


def sum_everywhere(value):
    for axis in ALL:
        count = lax.axis_size(axis)
        parts = [value]
        for k in range(1, count):
            parts.append(lax.ppermute(value, axis, [(i, i ^ k) for i in range(count)]))
        while len(parts) > 1:
            parts = [parts[i] + parts[i + 1] for i in range(0, len(parts), 2)]
        value = parts[0]
    return value


def update_kernel(scalars, in_ref, out_ref, resid_ref, direc_ref, resid_next, direc_next):
    for i, product in ((0, in_ref), (1, out_ref)):
        fresh = resid_ref[:, i, :] - scalars[0] * product[...].astype(jnp.float32)
        resid_next[:, i, :] = fresh
        direc_next[:, i, :] = fresh + scalars[1] * direc_ref[:, i, :]


def update(scalars, curved_in, curved_out, resid, direc, columns):
    rows, pair, total = resid.shape
    native = pl.BlockSpec((rows, pair, columns), lambda i: (0, 0, i))
    flat = pl.BlockSpec((rows, columns), lambda i: (0, i))
    return pl.pallas_call(
        update_kernel,
        grid=(total // columns,),
        in_specs=[pl.BlockSpec(memory_space=pltpu.SMEM), flat, flat, native, native],
        out_specs=[native, native],
        out_shape=[jax.ShapeDtypeStruct(resid.shape, jnp.float32)] * 2,
        compiler_params=pltpu.CompilerParams(vmem_limit_bytes=32 * 1024 * 1024),
        cost_estimate=pl.CostEstimate(
            flops=4 * resid.size, bytes_accessed=20 * resid.size, transcendentals=0
        ),
    )(scalars, curved_in, curved_out, resid, direc)


def apart(array):
    turned = with_layout_constraint(jnp.transpose(array, (1, 0, 2)), Layout((0, 1, 2)))
    return lax.optimization_barrier(turned)


def on_device(states, task_weights, pad_mask, direction, residual):
    sections = lax.axis_size("section")
    tasks = lax.axis_size("task")
    shards = lax.axis_size("fsdp")
    section_id = lax.axis_index("section")
    task_id = lax.axis_index("task")
    shard_id = lax.axis_index("fsdp")
    w_in = task_weights[0, 0, 0]
    w_out = task_weights[0, 0, 1]
    width, hidden = w_in.shape
    row_count = states.shape[1]
    joined = row_count * shards
    block = width // tasks
    piece = block // shards
    direc_local = direction[0]
    resid_local = residual[0]

    direc_apart = apart(direc_local)
    resid_apart = apart(resid_local)
    narrow = [direc_apart[i].astype(jnp.bfloat16) for i in range(2)]

    def direction_for(k):
        at = (shard_id ^ k) * hidden
        return jnp.stack([lax.dynamic_slice_in_dim(part, at, hidden, 1) for part in narrow])

    pieces = fsdp_partners(direction_for)

    own_inputs = [states[0]]
    rows_all = gather_rows(states[0], 0, 0)
    for layer in range(sections):
        normed = normalize(rows_all.astype(jnp.float32))
        normed_b = normed.astype(jnp.bfloat16)
        preact = dot(normed_b, w_in)
        acted, slope = jax.jvp(gelu_tanh, (preact,), (jnp.ones_like(preact),))
        acted_b = acted.astype(jnp.bfloat16)
        if layer + 1 < sections:
            mixed = across_hidden(acted_b, w_out)
            if layer == 0:
                mixed, pieces[1] = tie(mixed, pieces[1])
            mixed = scatter_sum(mixed, layer, 0)
            own_rows = (own_inputs[layer].astype(jnp.float32) + mixed).astype(jnp.bfloat16)
            if layer == 0:
                own_rows, pieces[2] = tie(own_rows, pieces[2])
            own_inputs.append(own_rows)
            arrived = gather_rows(own_rows, 0, layer + 1)
            if layer == 0:
                arrived, (pieces[3], resid_apart) = tie(arrived, (pieces[3], resid_apart))
            rows_all = jnp.where(section_id == layer + 1, arrived, rows_all)

    steering = in_order(pieces, shard_id, 1)
    steer_in, steer_out = steering[0], steering[1]

    def features_for(array):
        return lambda k: lax.dynamic_slice_in_dim(array, (task_id ^ k) * block, block, 1)

    normed_parts = task_partners(features_for(normed_b))
    acted_b, normed_parts = tie(acted_b, normed_parts)
    normed_tasks = jnp.concatenate(normed_parts, axis=0)
    acted_tasks = jnp.concatenate(task_partners(lambda k: acted_b), axis=0)
    steered_parts = dot(normed_tasks, steer_in).reshape(tasks, joined, hidden)
    steered = task_partners(
        lambda k: steered_parts[k] if k == 0 else steered_parts[k].astype(jnp.bfloat16)
    )
    steered = sum(part.astype(jnp.float32) for part in steered)
    turned_parts = across_hidden(acted_tasks, steer_out).astype(jnp.bfloat16)
    turned_parts = turned_parts.reshape(tasks, joined, block)
    turned = in_order(task_partners(lambda k: turned_parts[k]), task_id, 1).astype(jnp.float32)

    own_dot = jnp.zeros((row_count, width), jnp.bfloat16)
    for layer in range(sections):
        if layer == 0:
            preact_dot = steered
        else:
            dots_all = gather_rows(own_dot, 0, layer)
            normed_dot = jax.jvp(
                normalize, (rows_all.astype(jnp.float32),), (dots_all.astype(jnp.float32),)
            )[1]
            preact_dot = dot(normed_dot.astype(jnp.bfloat16), w_in) + steered
        acted_dot_b = (slope * preact_dot).astype(jnp.bfloat16)
        mixed_dot = scatter_sum(across_hidden(acted_dot_b, w_out) + turned, layer, 0)
        own_dot = (own_dot.astype(jnp.float32) + mixed_dot).astype(jnp.bfloat16)

    own_bar = own_dot * pad_mask[0][:, None].astype(jnp.bfloat16)
    bars_all = jnp.zeros((joined, width), jnp.bfloat16)
    for layer in reversed(range(sections)):
        arrived = gather_rows(own_bar, 0, layer)
        bars_all = jnp.where(section_id == layer, arrived, bars_all)
        preact_bar = (dot(bars_all, w_out) * slope).astype(jnp.bfloat16)
        if layer > 0:
            normed_bar = scatter_sum(across_hidden(preact_bar, w_in), layer, 0)
            pullback = jax.vjp(normalize, own_inputs[layer].astype(jnp.float32))[1]
            own_bar = (own_bar.astype(jnp.float32) + pullback(normed_bar)[0]).astype(jnp.bfloat16)

    def to_owners(curved):
        curved = curved.astype(jnp.bfloat16).reshape(shards, piece, hidden)

        def curved_for(k):
            return lax.dynamic_index_in_dim(curved, shard_id ^ k, 0, keepdims=False)

        return in_order(fsdp_partners(curved_for), shard_id, 1)

    bars_tasks = jnp.concatenate(task_partners(features_for(bars_all)), axis=0)
    curved_out = to_owners(across_tokens(bars_tasks, acted_tasks))
    preact_bars_tasks = jnp.concatenate(task_partners(lambda k: preact_bar), axis=0)
    curved_in = to_owners(across_tokens(normed_tasks, preact_bars_tasks))
    products = [curved.astype(jnp.float32) for curved in (curved_in, curved_out)]

    sums = sum_everywhere(
        jnp.stack(
            [
                jnp.sum(resid_apart * resid_apart),
                sum(jnp.sum(direc_apart[i] * products[i]) for i in range(2)),
                sum(jnp.sum(resid_apart[i] * products[i]) for i in range(2)),
                sum(jnp.sum(products[i] * products[i]) for i in range(2)),
            ]
        )
    )
    start_norm, curvature, crossed, squared = sums[0], sums[1], sums[2], sums[3]
    step_size = start_norm / curvature
    next_norm = start_norm - 2.0 * step_size * crossed + step_size * step_size * squared
    resid_next, direc_next = update(
        jnp.stack([step_size, next_norm / start_norm]),
        curved_in,
        curved_out,
        resid_local,
        direc_local,
        hidden,
    )
    return (resid_next[None], direc_next[None], step_size)


def solution(mesh):
    placed = (
        P("task", "fsdp", None),
        P("task", "section", None, None, "fsdp"),
        P("task", "fsdp"),
        P("section", ("task", "fsdp"), None, None),
        P("section", ("task", "fsdp"), None, None),
    )
    return jax.shard_map(
        on_device,
        mesh=mesh,
        in_specs=placed,
        out_specs=(
            P("section", ("task", "fsdp"), None, None),
            P("section", ("task", "fsdp"), None, None),
            P(),
        ),
        check_vma=False,
    )
```

```python
import jax
import jax.numpy as jnp
from jax import lax
from jax.experimental import pallas as pl
from jax.experimental.pallas import tpu as pltpu
from jax.experimental.layout import Layout, with_layout_constraint
from jax.sharding import PartitionSpec as P

ALL = ("section", "task", "fsdp")
eps_norm = 1e-06


def normalize(token_rows):
    return token_rows * lax.rsqrt(
        jnp.mean(token_rows * token_rows, axis=-1, keepdims=True) + eps_norm
    )


def gelu_tanh(values):
    return jax.nn.gelu(values, approximate=True)


def across_hidden(left_side, right_side):
    return lax.dot_general(
        left_side, right_side, (((1,), (1,)), ((), ())), preferred_element_type=jnp.float32
    )


def across_tokens(left_side, right_side):
    return lax.dot_general(
        left_side, right_side, (((0,), (0,)), ((), ())), preferred_element_type=jnp.float32
    )


def dot(left_side, right_side):
    return jnp.dot(left_side, right_side, preferred_element_type=jnp.float32)


def send(value, route):
    sections, tasks, shards = (lax.axis_size(axis) for axis in ALL)
    pairs = []
    for s in range(sections):
        for t in range(tasks):
            for f in range(shards):
                target = route(s, t, f)
                if target is not None:
                    to_s, to_t, to_f = target
                    pairs.append(
                        ((s * tasks + t) * shards + f, (to_s * tasks + to_t) * shards + to_f)
                    )
    return lax.ppermute(value, ALL, pairs)


def between(start, end, k):
    return lambda s, t, f: (end, t, f ^ k) if s == start else None


def gather_rows(rows, start, end):
    parts = []
    for k in range(lax.axis_size("fsdp")):
        if k == 0 and start == end:
            parts.append(rows)
        else:
            parts.append(send(rows, between(start, end, k)))
    return jnp.concatenate(parts, axis=0)


def scatter_sum(partial, start, end):
    shards = lax.axis_size("fsdp")
    blocks = partial.reshape(shards, partial.shape[0] // shards, partial.shape[1])
    total = None
    for k in range(shards):
        if k == 0 and start == end:
            part = blocks[0]
        else:
            part = send(blocks[k].astype(jnp.bfloat16), between(start, end, k)).astype(jnp.float32)
        total = part if total is None else total + part
    return total


def task_partners(value_of, section=None):
    def route(k):
        return lambda s, t, f: (s, t ^ k, f) if section in (None, s) else None

    parts = [value_of(0)]
    for k in range(1, lax.axis_size("task")):
        parts.append(send(value_of(k), route(k)))
    return parts


def fsdp_partners(value_of):
    parts = [value_of(0)]
    for k in range(1, lax.axis_size("fsdp")):
        parts.append(send(value_of(k), lambda s, t, f, k=k: (s, t, f ^ k)))
    return parts


def tie(value, other):
    return lax.optimization_barrier((value, other))


def in_order(parts, index, axis):
    stacked = jnp.stack(parts)
    return jnp.concatenate(
        [
            lax.dynamic_index_in_dim(stacked, index ^ j, 0, keepdims=False)
            for j in range(len(parts))
        ],
        axis=axis,
    )


def sum_everywhere(value):
    for axis in ALL:
        count = lax.axis_size(axis)
        parts = [value]
        for k in range(1, count):
            parts.append(lax.ppermute(value, axis, [(i, i ^ k) for i in range(count)]))
        while len(parts) > 1:
            parts = [parts[i] + parts[i + 1] for i in range(0, len(parts), 2)]
        value = parts[0]
    return value


def update_kernel(scalars, in_ref, out_ref, resid_ref, direc_ref, resid_next, direc_next):
    for i, product in ((0, in_ref), (1, out_ref)):
        fresh = resid_ref[:, i, :] - scalars[0] * product[...].astype(jnp.float32)
        resid_next[:, i, :] = fresh
        direc_next[:, i, :] = fresh + scalars[1] * direc_ref[:, i, :]


def update(scalars, curved_in, curved_out, resid, direc, columns):
    rows, pair, total = resid.shape
    native = pl.BlockSpec((rows, pair, columns), lambda i: (0, 0, i))
    flat = pl.BlockSpec((rows, columns), lambda i: (0, i))
    return pl.pallas_call(
        update_kernel,
        grid=(total // columns,),
        in_specs=[pl.BlockSpec(memory_space=pltpu.SMEM), flat, flat, native, native],
        out_specs=[native, native],
        out_shape=[jax.ShapeDtypeStruct(resid.shape, jnp.float32)] * 2,
        compiler_params=pltpu.CompilerParams(vmem_limit_bytes=32 * 1024 * 1024),
        cost_estimate=pl.CostEstimate(
            flops=4 * resid.size, bytes_accessed=20 * resid.size, transcendentals=0
        ),
    )(scalars, curved_in, curved_out, resid, direc)


def apart(array):
    turned = with_layout_constraint(jnp.transpose(array, (1, 0, 2)), Layout((0, 1, 2)))
    return lax.optimization_barrier(turned)


def on_device(states, task_weights, pad_mask, direction, residual):
    sections = lax.axis_size("section")
    tasks = lax.axis_size("task")
    shards = lax.axis_size("fsdp")
    section_id = lax.axis_index("section")
    task_id = lax.axis_index("task")
    shard_id = lax.axis_index("fsdp")
    w_in = task_weights[0, 0, 0]
    w_out = task_weights[0, 0, 1]
    width, hidden = w_in.shape
    row_count = states.shape[1]
    joined = row_count * shards
    block = width // tasks
    piece = block // shards
    direc_local = direction[0]
    resid_local = residual[0]

    direc_apart = apart(direc_local)
    resid_apart = apart(resid_local)
    narrow = [direc_apart[i].astype(jnp.bfloat16) for i in range(2)]

    def direction_for(k):
        at = (shard_id ^ k) * hidden
        return jnp.stack([lax.dynamic_slice_in_dim(part, at, hidden, 1) for part in narrow])

    pieces = fsdp_partners(direction_for)

    def features_for(array):
        return lambda k: lax.dynamic_slice_in_dim(array, (task_id ^ k) * block, block, 1)

    own_inputs = [states[0]]
    early = []
    rows_all = gather_rows(states[0], 0, 0)
    for layer in range(sections):
        normed = normalize(rows_all.astype(jnp.float32))
        normed_b = normed.astype(jnp.bfloat16)
        preact = dot(normed_b, w_in)
        acted, slope = jax.jvp(gelu_tanh, (preact,), (jnp.ones_like(preact),))
        acted_b = acted.astype(jnp.bfloat16)
        if layer + 1 < sections:
            early.append(
                task_partners(
                    lambda k: jnp.concatenate([features_for(normed_b)(k), acted_b], axis=1), layer
                )
            )
            mixed = across_hidden(acted_b, w_out)
            if layer == 0:
                mixed, pieces[1] = tie(mixed, pieces[1])
            mixed = scatter_sum(mixed, layer, 0)
            own_rows = (own_inputs[layer].astype(jnp.float32) + mixed).astype(jnp.bfloat16)
            if layer == 0:
                own_rows, (pieces[2], resid_apart) = tie(own_rows, (pieces[2], resid_apart))
            own_rows, early[layer] = tie(own_rows, early[layer])
            own_inputs.append(own_rows)
            arrived = gather_rows(own_rows, 0, layer + 1)
            if layer == 0:
                arrived, pieces[3] = tie(arrived, pieces[3])
            rows_all = jnp.where(section_id == layer + 1, arrived, rows_all)

    steering = in_order(pieces, shard_id, 1)
    steer_in, steer_out = steering[0], steering[1]

    normed_parts = task_partners(features_for(normed_b), sections - 1)
    acted_b, normed_parts = tie(acted_b, normed_parts)
    acted_parts = task_partners(lambda k: acted_b, sections - 1)
    for layer in range(sections - 1):
        for k in range(1, tasks):
            here = section_id == layer
            normed_parts[k] = jnp.where(here, early[layer][k][:, :block], normed_parts[k])
            acted_parts[k] = jnp.where(here, early[layer][k][:, block:], acted_parts[k])
    normed_tasks = jnp.concatenate(normed_parts, axis=0)
    acted_tasks = jnp.concatenate(acted_parts, axis=0)
    steered_parts = dot(normed_tasks, steer_in).reshape(tasks, joined, hidden)
    steered = task_partners(
        lambda k: steered_parts[k] if k == 0 else steered_parts[k].astype(jnp.bfloat16)
    )
    steered = sum(part.astype(jnp.float32) for part in steered)
    turned_parts = across_hidden(acted_tasks, steer_out).astype(jnp.bfloat16)
    turned_parts = turned_parts.reshape(tasks, joined, block)
    turned = in_order(task_partners(lambda k: turned_parts[k]), task_id, 1).astype(jnp.float32)

    own_dot = jnp.zeros((row_count, width), jnp.bfloat16)
    for layer in range(sections):
        if layer == 0:
            preact_dot = steered
        else:
            dots_all = gather_rows(own_dot, 0, layer)
            normed_dot = jax.jvp(
                normalize, (rows_all.astype(jnp.float32),), (dots_all.astype(jnp.float32),)
            )[1]
            preact_dot = dot(normed_dot.astype(jnp.bfloat16), w_in) + steered
        acted_dot_b = (slope * preact_dot).astype(jnp.bfloat16)
        mixed_dot = scatter_sum(across_hidden(acted_dot_b, w_out) + turned, layer, 0)
        own_dot = (own_dot.astype(jnp.float32) + mixed_dot).astype(jnp.bfloat16)

    own_bar = own_dot * pad_mask[0][:, None].astype(jnp.bfloat16)
    bars_all = jnp.zeros((joined, width), jnp.bfloat16)
    for layer in reversed(range(sections)):
        arrived = gather_rows(own_bar, 0, layer)
        bars_all = jnp.where(section_id == layer, arrived, bars_all)
        preact_bar = (dot(bars_all, w_out) * slope).astype(jnp.bfloat16)
        if layer > 0:
            normed_bar = scatter_sum(across_hidden(preact_bar, w_in), layer, 0)
            pullback = jax.vjp(normalize, own_inputs[layer].astype(jnp.float32))[1]
            own_bar = (own_bar.astype(jnp.float32) + pullback(normed_bar)[0]).astype(jnp.bfloat16)

    def to_owners(curved):
        curved = curved.astype(jnp.bfloat16).reshape(shards, piece, hidden)

        def curved_for(k):
            return lax.dynamic_index_in_dim(curved, shard_id ^ k, 0, keepdims=False)

        return in_order(fsdp_partners(curved_for), shard_id, 1)

    bars_tasks = jnp.concatenate(task_partners(features_for(bars_all)), axis=0)
    curved_out = to_owners(across_tokens(bars_tasks, acted_tasks))
    preact_bars_tasks = jnp.concatenate(task_partners(lambda k: preact_bar), axis=0)
    curved_in = to_owners(across_tokens(normed_tasks, preact_bars_tasks))
    products = [curved.astype(jnp.float32) for curved in (curved_in, curved_out)]

    sums = sum_everywhere(
        jnp.stack(
            [
                jnp.sum(resid_apart * resid_apart),
                sum(jnp.sum(direc_apart[i] * products[i]) for i in range(2)),
                sum(jnp.sum(resid_apart[i] * products[i]) for i in range(2)),
                sum(jnp.sum(products[i] * products[i]) for i in range(2)),
            ]
        )
    )
    start_norm, curvature, crossed, squared = sums[0], sums[1], sums[2], sums[3]
    step_size = start_norm / curvature
    next_norm = start_norm - 2.0 * step_size * crossed + step_size * step_size * squared
    resid_next, direc_next = update(
        jnp.stack([step_size, next_norm / start_norm]),
        curved_in,
        curved_out,
        resid_local,
        direc_local,
        hidden,
    )
    return (resid_next[None], direc_next[None], step_size)


def solution(mesh):
    placed = (
        P("task", "fsdp", None),
        P("task", "section", None, None, "fsdp"),
        P("task", "fsdp"),
        P("section", ("task", "fsdp"), None, None),
        P("section", ("task", "fsdp"), None, None),
    )
    return jax.shard_map(
        on_device,
        mesh=mesh,
        in_specs=placed,
        out_specs=(
            P("section", ("task", "fsdp"), None, None),
            P("section", ("task", "fsdp"), None, None),
            P(),
        ),
        check_vma=False,
    )
```

```python
import jax
import jax.numpy as jnp
from jax import lax
from jax.experimental import pallas as pl
from jax.experimental.pallas import tpu as pltpu
from jax.experimental.layout import Layout, with_layout_constraint
from jax.sharding import PartitionSpec as P

ALL = ("section", "task", "fsdp")
eps_norm = 1e-06


def normalize(token_rows):
    return token_rows * lax.rsqrt(
        jnp.mean(token_rows * token_rows, axis=-1, keepdims=True) + eps_norm
    )


def gelu_tanh(values):
    return jax.nn.gelu(values, approximate=True)


def across_hidden(left_side, right_side):
    return lax.dot_general(
        left_side, right_side, (((1,), (1,)), ((), ())), preferred_element_type=jnp.float32
    )


def across_tokens(left_side, right_side):
    return lax.dot_general(
        left_side, right_side, (((0,), (0,)), ((), ())), preferred_element_type=jnp.float32
    )


def dot(left_side, right_side):
    return jnp.dot(left_side, right_side, preferred_element_type=jnp.float32)


def send(value, route):
    sections, tasks, shards = (lax.axis_size(axis) for axis in ALL)
    pairs = []
    for s in range(sections):
        for t in range(tasks):
            for f in range(shards):
                target = route(s, t, f)
                if target is not None:
                    to_s, to_t, to_f = target
                    pairs.append(
                        ((s * tasks + t) * shards + f, (to_s * tasks + to_t) * shards + to_f)
                    )
    return lax.ppermute(value, ALL, pairs)


def between(start, end, k):
    return lambda s, t, f: (end, t, f ^ k) if s == start else None


def gather_rows(rows, start, end):
    parts = []
    for k in range(lax.axis_size("fsdp")):
        if k == 0 and start == end:
            parts.append(rows)
        else:
            parts.append(send(rows, between(start, end, k)))
    return jnp.concatenate(parts, axis=0)


def scatter_sum(partial, start, end):
    shards = lax.axis_size("fsdp")
    blocks = partial.reshape(shards, partial.shape[0] // shards, partial.shape[1])
    total = None
    for k in range(shards):
        if k == 0 and start == end:
            part = blocks[0]
        else:
            part = send(blocks[k].astype(jnp.bfloat16), between(start, end, k)).astype(jnp.float32)
        total = part if total is None else total + part
    return total


def task_partners(value_of, section=None):
    def route(k):
        return lambda s, t, f: (s, t ^ k, f) if section in (None, s) else None

    parts = [value_of(0)]
    for k in range(1, lax.axis_size("task")):
        parts.append(send(value_of(k), route(k)))
    return parts


def fsdp_partners(value_of):
    parts = [value_of(0)]
    for k in range(1, lax.axis_size("fsdp")):
        parts.append(send(value_of(k), lambda s, t, f, k=k: (s, t, f ^ k)))
    return parts


def tie(value, other):
    return lax.optimization_barrier((value, other))


def in_order(parts, index, axis):
    stacked = jnp.stack(parts)
    return jnp.concatenate(
        [
            lax.dynamic_index_in_dim(stacked, index ^ j, 0, keepdims=False)
            for j in range(len(parts))
        ],
        axis=axis,
    )


def sum_everywhere(value):
    for axis in ALL:
        count = lax.axis_size(axis)
        parts = [value]
        for k in range(1, count):
            parts.append(lax.ppermute(value, axis, [(i, i ^ k) for i in range(count)]))
        while len(parts) > 1:
            parts = [parts[i] + parts[i + 1] for i in range(0, len(parts), 2)]
        value = parts[0]
    return value


def update_kernel(scalars, in_ref, out_ref, resid_ref, direc_ref, resid_next, direc_next):
    for i, product in ((0, in_ref), (1, out_ref)):
        fresh = resid_ref[:, i, :] - scalars[0] * product[...].astype(jnp.float32)
        resid_next[:, i, :] = fresh
        direc_next[:, i, :] = fresh + scalars[1] * direc_ref[:, i, :]


def update(scalars, curved_in, curved_out, resid, direc, columns):
    rows, pair, total = resid.shape
    native = pl.BlockSpec((rows, pair, columns), lambda i: (0, 0, i))
    flat = pl.BlockSpec((rows, columns), lambda i: (0, i))
    return pl.pallas_call(
        update_kernel,
        grid=(total // columns,),
        in_specs=[pl.BlockSpec(memory_space=pltpu.SMEM), flat, flat, native, native],
        out_specs=[native, native],
        out_shape=[jax.ShapeDtypeStruct(resid.shape, jnp.float32)] * 2,
        compiler_params=pltpu.CompilerParams(vmem_limit_bytes=32 * 1024 * 1024),
        cost_estimate=pl.CostEstimate(
            flops=4 * resid.size, bytes_accessed=20 * resid.size, transcendentals=0
        ),
    )(scalars, curved_in, curved_out, resid, direc)


def apart(array):
    turned = with_layout_constraint(jnp.transpose(array, (1, 0, 2)), Layout((0, 1, 2)))
    return lax.optimization_barrier(turned)


def on_device(states, task_weights, pad_mask, direction, residual):
    sections = lax.axis_size("section")
    tasks = lax.axis_size("task")
    shards = lax.axis_size("fsdp")
    section_id = lax.axis_index("section")
    task_id = lax.axis_index("task")
    shard_id = lax.axis_index("fsdp")
    w_in = task_weights[0, 0, 0]
    w_out = task_weights[0, 0, 1]
    width, hidden = w_in.shape
    row_count = states.shape[1]
    joined = row_count * shards
    block = width // tasks
    piece = block // shards
    direc_local = direction[0]
    resid_local = residual[0]

    direc_apart = apart(direc_local)
    resid_apart = apart(resid_local)
    narrow = [direc_apart[i].astype(jnp.bfloat16) for i in range(2)]

    def direction_for(k):
        at = (shard_id ^ k) * hidden
        return jnp.stack([lax.dynamic_slice_in_dim(part, at, hidden, 1) for part in narrow])

    pieces = fsdp_partners(direction_for)

    def features_for(array):
        return lambda k: lax.dynamic_slice_in_dim(array, (task_id ^ k) * block, block, 1)

    own_inputs = [states[0]]
    packed = []
    rows_all = gather_rows(states[0], 0, 0)
    for layer in range(sections):
        normed = normalize(rows_all.astype(jnp.float32))
        normed_b = normed.astype(jnp.bfloat16)
        preact = dot(normed_b, w_in)
        acted, slope = jax.jvp(gelu_tanh, (preact,), (jnp.ones_like(preact),))
        acted_b = acted.astype(jnp.bfloat16)
        packed.append(
            task_partners(
                lambda k: jnp.concatenate([features_for(normed_b)(k), acted_b], axis=1), layer
            )
        )
        if layer + 1 < sections:
            mixed = across_hidden(acted_b, w_out)
            mixed = scatter_sum(mixed, layer, 0)
            own_rows = (own_inputs[layer].astype(jnp.float32) + mixed).astype(jnp.bfloat16)
            if layer == 0:
                own_rows, pieces[1:3] = tie(own_rows, pieces[1:3])
            own_rows, packed[layer] = tie(own_rows, packed[layer])
            own_inputs.append(own_rows)
            arrived = gather_rows(own_rows, 0, layer + 1)
            if layer == 0:
                arrived, pieces[3] = tie(arrived, pieces[3])
            rows_all = jnp.where(section_id == layer + 1, arrived, rows_all)

    steering = in_order(pieces, shard_id, 1)
    steer_in, steer_out = steering[0], steering[1]

    parts = packed[-1]
    for layer in range(sections - 1):
        here = section_id == layer
        for k in range(1, tasks):
            parts[k] = jnp.where(here, packed[layer][k], parts[k])
    normed_tasks = jnp.concatenate([part[:, :block] for part in parts], axis=0)
    acted_tasks = jnp.concatenate([part[:, block:] for part in parts], axis=0)
    steered_parts = dot(normed_tasks, steer_in).reshape(tasks, joined, hidden)
    turned_parts = across_hidden(acted_tasks, steer_out).reshape(tasks, joined, block)
    parts = task_partners(
        lambda k: jnp.concatenate(
            [
                steered_parts[k].astype(jnp.bfloat16),
                turned_parts[k].astype(jnp.bfloat16),
            ],
            axis=1,
        )
    )
    parts, resid_apart = tie(parts, resid_apart)
    steered = sum((part[:, :hidden].astype(jnp.float32) for part in parts[1:]), steered_parts[0])
    turned = in_order([part[:, hidden:] for part in parts], task_id, 1).astype(jnp.float32)

    own_dot = jnp.zeros((row_count, width), jnp.bfloat16)
    for layer in range(sections):
        if layer == 0:
            preact_dot = steered
        else:
            dots_all = gather_rows(own_dot, 0, layer)
            normed_dot = jax.jvp(
                normalize, (rows_all.astype(jnp.float32),), (dots_all.astype(jnp.float32),)
            )[1]
            preact_dot = dot(normed_dot.astype(jnp.bfloat16), w_in) + steered
        acted_dot_b = (slope * preact_dot).astype(jnp.bfloat16)
        mixed_dot = scatter_sum(across_hidden(acted_dot_b, w_out) + turned, layer, 0)
        own_dot = (own_dot.astype(jnp.float32) + mixed_dot).astype(jnp.bfloat16)

    own_bar = own_dot * pad_mask[0][:, None].astype(jnp.bfloat16)
    bars_all = jnp.zeros((joined, width), jnp.bfloat16)
    for layer in reversed(range(sections)):
        arrived = gather_rows(own_bar, 0, layer)
        bars_all = jnp.where(section_id == layer, arrived, bars_all)
        preact_bar = (dot(bars_all, w_out) * slope).astype(jnp.bfloat16)
        if layer > 0:
            normed_bar = scatter_sum(across_hidden(preact_bar, w_in), layer, 0)
            pullback = jax.vjp(normalize, own_inputs[layer].astype(jnp.float32))[1]
            own_bar = (own_bar.astype(jnp.float32) + pullback(normed_bar)[0]).astype(jnp.bfloat16)

    def to_owners(curved):
        curved = curved.astype(jnp.bfloat16).reshape(shards, piece, hidden)

        def curved_for(k):
            return lax.dynamic_index_in_dim(curved, shard_id ^ k, 0, keepdims=False)

        return in_order(fsdp_partners(curved_for), shard_id, 1)

    bars_tasks = jnp.concatenate(task_partners(features_for(bars_all)), axis=0)
    curved_out = to_owners(across_tokens(bars_tasks, acted_tasks))
    preact_bars_tasks = jnp.concatenate(task_partners(lambda k: preact_bar), axis=0)
    curved_in = to_owners(across_tokens(normed_tasks, preact_bars_tasks))
    products = [curved.astype(jnp.float32) for curved in (curved_in, curved_out)]

    sums = sum_everywhere(
        jnp.stack(
            [
                jnp.sum(resid_apart * resid_apart),
                sum(jnp.sum(direc_apart[i] * products[i]) for i in range(2)),
                sum(jnp.sum(resid_apart[i] * products[i]) for i in range(2)),
                sum(jnp.sum(products[i] * products[i]) for i in range(2)),
            ]
        )
    )
    start_norm, curvature, crossed, squared = sums[0], sums[1], sums[2], sums[3]
    step_size = start_norm / curvature
    next_norm = start_norm - 2.0 * step_size * crossed + step_size * step_size * squared
    resid_next, direc_next = update(
        jnp.stack([step_size, next_norm / start_norm]),
        curved_in,
        curved_out,
        resid_local,
        direc_local,
        hidden,
    )
    return (resid_next[None], direc_next[None], step_size)


def solution(mesh):
    placed = (
        P("task", "fsdp", None),
        P("task", "section", None, None, "fsdp"),
        P("task", "fsdp"),
        P("section", ("task", "fsdp"), None, None),
        P("section", ("task", "fsdp"), None, None),
    )
    return jax.shard_map(
        on_device,
        mesh=mesh,
        in_specs=placed,
        out_specs=(
            P("section", ("task", "fsdp"), None, None),
            P("section", ("task", "fsdp"), None, None),
            P(),
        ),
        check_vma=False,
    )
```

```python
import jax
import jax.numpy as jnp
from jax import lax
from jax.experimental import pallas as pl
from jax.experimental.pallas import tpu as pltpu
from jax.experimental.layout import Layout, with_layout_constraint
from jax.sharding import PartitionSpec as P

ALL = ("section", "task", "fsdp")
eps_norm = 1e-06


def normalize(token_rows):
    return token_rows * lax.rsqrt(
        jnp.mean(token_rows * token_rows, axis=-1, keepdims=True) + eps_norm
    )


def gelu_tanh(values):
    return jax.nn.gelu(values, approximate=True)


def across_hidden(left_side, right_side):
    return lax.dot_general(
        left_side, right_side, (((1,), (1,)), ((), ())), preferred_element_type=jnp.float32
    )


def across_tokens(left_side, right_side):
    return lax.dot_general(
        left_side, right_side, (((0,), (0,)), ((), ())), preferred_element_type=jnp.float32
    )


def dot(left_side, right_side):
    return jnp.dot(left_side, right_side, preferred_element_type=jnp.float32)


def send(value, route):
    sections, tasks, shards = (lax.axis_size(axis) for axis in ALL)
    pairs = []
    for s in range(sections):
        for t in range(tasks):
            for f in range(shards):
                target = route(s, t, f)
                if target is not None:
                    to_s, to_t, to_f = target
                    pairs.append(
                        ((s * tasks + t) * shards + f, (to_s * tasks + to_t) * shards + to_f)
                    )
    return lax.ppermute(value, ALL, pairs)


def between(start, end, k):
    return lambda s, t, f: (end, t, f ^ k) if s == start else None


def gather_rows(rows, start, end):
    parts = []
    for k in range(lax.axis_size("fsdp")):
        if k == 0 and start == end:
            parts.append(rows)
        else:
            parts.append(send(rows, between(start, end, k)))
    return jnp.concatenate(parts, axis=0)


def scatter_sum(partial, start, end):
    shards = lax.axis_size("fsdp")
    blocks = partial.reshape(shards, partial.shape[0] // shards, partial.shape[1])
    total = None
    for k in range(shards):
        if k == 0 and start == end:
            part = blocks[0]
        else:
            part = send(blocks[k].astype(jnp.bfloat16), between(start, end, k)).astype(jnp.float32)
        total = part if total is None else total + part
    return total


def task_partners(value_of, section=None):
    def route(k):
        return lambda s, t, f: (s, t ^ k, f) if section in (None, s) else None

    parts = [value_of(0)]
    for k in range(1, lax.axis_size("task")):
        parts.append(send(value_of(k), route(k)))
    return parts


def fsdp_partners(value_of):
    parts = [value_of(0)]
    for k in range(1, lax.axis_size("fsdp")):
        parts.append(send(value_of(k), lambda s, t, f, k=k: (s, t, f ^ k)))
    return parts


def tie(value, other):
    return lax.optimization_barrier((value, other))


def in_order(parts, index, axis):
    stacked = jnp.stack(parts)
    return jnp.concatenate(
        [
            lax.dynamic_index_in_dim(stacked, index ^ j, 0, keepdims=False)
            for j in range(len(parts))
        ],
        axis=axis,
    )


def sum_everywhere(value):
    for axis in ALL:
        count = lax.axis_size(axis)
        parts = [value]
        for k in range(1, count):
            parts.append(lax.ppermute(value, axis, [(i, i ^ k) for i in range(count)]))
        while len(parts) > 1:
            parts = [parts[i] + parts[i + 1] for i in range(0, len(parts), 2)]
        value = parts[0]
    return value


def update_kernel(sums_ref, in_ref, out_ref, resid_ref, direc_ref, resid_next, direc_next, step_ref):
    start_norm, curvature, crossed, squared = (
        jnp.sum(sums_ref[i : i + 1, :], axis=1, keepdims=True) for i in range(4)
    )
    step_size = start_norm / curvature
    next_norm = start_norm - 2.0 * step_size * crossed + step_size * step_size * squared
    ratio = next_norm / start_norm
    step_ref[...] = step_size
    for i, product in ((0, in_ref), (1, out_ref)):
        fresh = resid_ref[:, i, :] - step_size * product[...].astype(jnp.float32)
        resid_next[:, i, :] = fresh
        direc_next[:, i, :] = fresh + ratio * direc_ref[:, i, :]


def update(sums, curved_in, curved_out, resid, direc, columns):
    rows, pair, total = resid.shape
    native = pl.BlockSpec((rows, pair, columns), lambda i: (0, 0, i))
    flat = pl.BlockSpec((rows, columns), lambda i: (0, i))
    return pl.pallas_call(
        update_kernel,
        grid=(total // columns,),
        in_specs=[pl.BlockSpec(sums.shape, lambda i: (0, 0)), flat, flat, native, native],
        out_specs=[native, native, pl.BlockSpec((1, 1), lambda i: (0, 0))],
        out_shape=[jax.ShapeDtypeStruct(resid.shape, jnp.float32)] * 2
        + [jax.ShapeDtypeStruct((1, 1), jnp.float32)],
        compiler_params=pltpu.CompilerParams(vmem_limit_bytes=58 * 1024 * 1024),
        cost_estimate=pl.CostEstimate(
            flops=4 * resid.size, bytes_accessed=20 * resid.size, transcendentals=0
        ),
    )(sums, curved_in, curved_out, resid, direc)


def apart(array):
    turned = with_layout_constraint(jnp.transpose(array, (1, 0, 2)), Layout((0, 1, 2)))
    return lax.optimization_barrier(turned)


def on_device(states, task_weights, pad_mask, direction, residual):
    sections = lax.axis_size("section")
    tasks = lax.axis_size("task")
    shards = lax.axis_size("fsdp")
    section_id = lax.axis_index("section")
    task_id = lax.axis_index("task")
    shard_id = lax.axis_index("fsdp")
    w_in = task_weights[0, 0, 0]
    w_out = task_weights[0, 0, 1]
    width, hidden = w_in.shape
    row_count = states.shape[1]
    joined = row_count * shards
    block = width // tasks
    piece = block // shards
    direc_local = direction[0]
    resid_local = residual[0]

    direc_apart = apart(direc_local)
    resid_apart = apart(resid_local)
    narrow = [direc_apart[i].astype(jnp.bfloat16) for i in range(2)]

    def direction_for(k):
        at = (shard_id ^ k) * hidden
        return jnp.stack([lax.dynamic_slice_in_dim(part, at, hidden, 1) for part in narrow])

    pieces = fsdp_partners(direction_for)

    def features_for(array):
        return lambda k: lax.dynamic_slice_in_dim(array, (task_id ^ k) * block, block, 1)

    own_inputs = [states[0]]
    packed = []
    rows_all = gather_rows(states[0], 0, 0)
    for layer in range(sections):
        normed = normalize(rows_all.astype(jnp.float32))
        normed_b = normed.astype(jnp.bfloat16)
        preact = dot(normed_b, w_in)
        acted, slope = jax.jvp(gelu_tanh, (preact,), (jnp.ones_like(preact),))
        acted_b = acted.astype(jnp.bfloat16)
        packed.append(
            task_partners(
                lambda k: jnp.concatenate([features_for(normed_b)(k), acted_b], axis=1), layer
            )
        )
        if layer + 1 < sections:
            mixed = across_hidden(acted_b, w_out)
            mixed = scatter_sum(mixed, layer, 0)
            own_rows = (own_inputs[layer].astype(jnp.float32) + mixed).astype(jnp.bfloat16)
            if layer == 0:
                own_rows, pieces[1:3] = tie(own_rows, pieces[1:3])
            own_rows, packed[layer] = tie(own_rows, packed[layer])
            own_inputs.append(own_rows)
            arrived = gather_rows(own_rows, 0, layer + 1)
            if layer == 0:
                arrived, pieces[3] = tie(arrived, pieces[3])
            rows_all = jnp.where(section_id == layer + 1, arrived, rows_all)

    steering = in_order(pieces, shard_id, 1)
    steer_in, steer_out = steering[0], steering[1]

    parts = packed[-1]
    for layer in range(sections - 1):
        here = section_id == layer
        for k in range(1, tasks):
            parts[k] = jnp.where(here, packed[layer][k], parts[k])
    normed_tasks = jnp.concatenate([part[:, :block] for part in parts], axis=0)
    acted_tasks = jnp.concatenate([part[:, block:] for part in parts], axis=0)
    steered_parts = dot(normed_tasks, steer_in).reshape(tasks, joined, hidden)
    turned_parts = across_hidden(acted_tasks, steer_out).reshape(tasks, joined, block)
    parts = task_partners(
        lambda k: jnp.concatenate(
            [
                steered_parts[k].astype(jnp.bfloat16),
                turned_parts[k].astype(jnp.bfloat16),
            ],
            axis=1,
        )
    )
    parts, resid_apart = tie(parts, resid_apart)
    steered = sum((part[:, :hidden].astype(jnp.float32) for part in parts[1:]), steered_parts[0])
    turned = in_order([part[:, hidden:] for part in parts], task_id, 1).astype(jnp.float32)

    own_dot = jnp.zeros((row_count, width), jnp.bfloat16)
    for layer in range(sections):
        if layer == 0:
            preact_dot = steered
        else:
            dots_all = gather_rows(own_dot, 0, layer)
            normed_dot = jax.jvp(
                normalize, (rows_all.astype(jnp.float32),), (dots_all.astype(jnp.float32),)
            )[1]
            preact_dot = dot(normed_dot.astype(jnp.bfloat16), w_in) + steered
        acted_dot_b = (slope * preact_dot).astype(jnp.bfloat16)
        mixed_dot = scatter_sum(across_hidden(acted_dot_b, w_out) + turned, layer, 0)
        own_dot = (own_dot.astype(jnp.float32) + mixed_dot).astype(jnp.bfloat16)

    own_bar = own_dot * pad_mask[0][:, None].astype(jnp.bfloat16)
    bars_all = jnp.zeros((joined, width), jnp.bfloat16)
    for layer in reversed(range(sections)):
        arrived = gather_rows(own_bar, 0, layer)
        bars_all = jnp.where(section_id == layer, arrived, bars_all)
        preact_bar = (dot(bars_all, w_out) * slope).astype(jnp.bfloat16)
        if layer > 0:
            normed_bar = scatter_sum(across_hidden(preact_bar, w_in), layer, 0)
            pullback = jax.vjp(normalize, own_inputs[layer].astype(jnp.float32))[1]
            own_bar = (own_bar.astype(jnp.float32) + pullback(normed_bar)[0]).astype(jnp.bfloat16)

    def to_owners(curved):
        curved = curved.astype(jnp.bfloat16).reshape(shards, piece, hidden)

        def curved_for(k):
            return lax.dynamic_index_in_dim(curved, shard_id ^ k, 0, keepdims=False)

        return in_order(fsdp_partners(curved_for), shard_id, 1)

    bars_tasks = jnp.concatenate(task_partners(features_for(bars_all)), axis=0)
    curved_out = to_owners(across_tokens(bars_tasks, acted_tasks))
    preact_bars_tasks = jnp.concatenate(task_partners(lambda k: preact_bar), axis=0)
    curved_in = to_owners(across_tokens(normed_tasks, preact_bars_tasks))
    products = [curved.astype(jnp.float32) for curved in (curved_in, curved_out)]

    def folded(values):
        blocks = [
            value[:, i * hidden : (i + 1) * hidden] for value in values for i in range(shards)
        ]
        return jnp.sum(sum(blocks), axis=0)

    sums = sum_everywhere(
        jnp.stack(
            [
                folded([resid_apart[i] * resid_apart[i] for i in range(2)]),
                folded([direc_apart[i] * products[i] for i in range(2)]),
                folded([resid_apart[i] * products[i] for i in range(2)]),
                folded([products[i] * products[i] for i in range(2)]),
            ]
        )
    )
    resid_next, direc_next, step_size = update(
        sums, curved_in, curved_out, resid_local, direc_local, hidden
    )
    return (resid_next[None], direc_next[None], step_size[0, 0])


def solution(mesh):
    placed = (
        P("task", "fsdp", None),
        P("task", "section", None, None, "fsdp"),
        P("task", "fsdp"),
        P("section", ("task", "fsdp"), None, None),
        P("section", ("task", "fsdp"), None, None),
    )
    return jax.shard_map(
        on_device,
        mesh=mesh,
        in_specs=placed,
        out_specs=(
            P("section", ("task", "fsdp"), None, None),
            P("section", ("task", "fsdp"), None, None),
            P(),
        ),
        check_vma=False,
    )
```

```python
import jax
import jax.numpy as jnp
from jax import lax
from jax.experimental import pallas as pl
from jax.experimental.pallas import tpu as pltpu
from jax.experimental.layout import Layout, with_layout_constraint
from jax.sharding import PartitionSpec as P

ALL = ("section", "task", "fsdp")
eps_norm = 1e-06


def normalize(token_rows):
    return token_rows * lax.rsqrt(
        jnp.mean(token_rows * token_rows, axis=-1, keepdims=True) + eps_norm
    )


def gelu_tanh(values):
    return jax.nn.gelu(values, approximate=True)


def across_hidden(left_side, right_side):
    return lax.dot_general(
        left_side, right_side, (((1,), (1,)), ((), ())), preferred_element_type=jnp.float32
    )


def across_tokens(left_side, right_side):
    return lax.dot_general(
        left_side, right_side, (((0,), (0,)), ((), ())), preferred_element_type=jnp.float32
    )


def dot(left_side, right_side):
    return jnp.dot(left_side, right_side, preferred_element_type=jnp.float32)


def send(value, route):
    sections, tasks, shards = (lax.axis_size(axis) for axis in ALL)
    pairs = []
    for s in range(sections):
        for t in range(tasks):
            for f in range(shards):
                target = route(s, t, f)
                if target is not None:
                    to_s, to_t, to_f = target
                    pairs.append(
                        ((s * tasks + t) * shards + f, (to_s * tasks + to_t) * shards + to_f)
                    )
    return lax.ppermute(value, ALL, pairs)


def between(start, end, k):
    return lambda s, t, f: (end, t, f ^ k) if s == start else None


def gather_rows(rows, start, end):
    parts = []
    for k in range(lax.axis_size("fsdp")):
        if k == 0 and start == end:
            parts.append(rows)
        else:
            parts.append(send(rows, between(start, end, k)))
    return jnp.concatenate(parts, axis=0)


def scatter_sum(partial, start, end):
    shards = lax.axis_size("fsdp")
    blocks = partial.reshape(shards, partial.shape[0] // shards, partial.shape[1])
    total = None
    for k in range(shards):
        if k == 0 and start == end:
            part = blocks[0]
        else:
            part = send(blocks[k].astype(jnp.bfloat16), between(start, end, k)).astype(jnp.float32)
        total = part if total is None else total + part
    return total


def task_partners(value_of, section=None):
    def route(k):
        return lambda s, t, f: (s, t ^ k, f) if section in (None, s) else None

    parts = [value_of(0)]
    for k in range(1, lax.axis_size("task")):
        parts.append(send(value_of(k), route(k)))
    return parts


def across(k, held_by):
    return lambda s, t, f: (s, t, f ^ k) if s in held_by else None


def fsdp_partners(value_of):
    parts = [value_of(0)]
    for k in range(1, lax.axis_size("fsdp")):
        parts.append(send(value_of(k), lambda s, t, f, k=k: (s, t, f ^ k)))
    return parts


def tie(value, other):
    return lax.optimization_barrier((value, other))


def in_order(parts, index, axis):
    stacked = jnp.stack(parts)
    return jnp.concatenate(
        [
            lax.dynamic_index_in_dim(stacked, index ^ j, 0, keepdims=False)
            for j in range(len(parts))
        ],
        axis=axis,
    )


def sum_everywhere(value):
    for axis in ALL:
        count = lax.axis_size(axis)
        parts = [value]
        for k in range(1, count):
            parts.append(lax.ppermute(value, axis, [(i, i ^ k) for i in range(count)]))
        while len(parts) > 1:
            parts = [parts[i] + parts[i + 1] for i in range(0, len(parts), 2)]
        value = parts[0]
    return value


def update_kernel(sums_ref, in_ref, out_ref, resid_ref, direc_ref, resid_next, direc_next, step_ref):
    start_norm, curvature, crossed, squared = (
        jnp.sum(sums_ref[i : i + 1, :], axis=1, keepdims=True) for i in range(4)
    )
    step_size = start_norm / curvature
    next_norm = start_norm - 2.0 * step_size * crossed + step_size * step_size * squared
    ratio = next_norm / start_norm
    step_ref[...] = step_size
    for i, product in ((0, in_ref), (1, out_ref)):
        fresh = resid_ref[:, i, :] - step_size * product[...].astype(jnp.float32)
        resid_next[:, i, :] = fresh
        direc_next[:, i, :] = fresh + ratio * direc_ref[:, i, :]


def update(sums, curved_in, curved_out, resid, direc, columns):
    rows, pair, total = resid.shape
    native = pl.BlockSpec((rows, pair, columns), lambda i: (0, 0, i))
    flat = pl.BlockSpec((rows, columns), lambda i: (0, i))
    return pl.pallas_call(
        update_kernel,
        grid=(total // columns,),
        in_specs=[pl.BlockSpec(sums.shape, lambda i: (0, 0)), flat, flat, native, native],
        out_specs=[native, native, pl.BlockSpec((1, 1), lambda i: (0, 0))],
        out_shape=[jax.ShapeDtypeStruct(resid.shape, jnp.float32)] * 2
        + [jax.ShapeDtypeStruct((1, 1), jnp.float32)],
        compiler_params=pltpu.CompilerParams(vmem_limit_bytes=58 * 1024 * 1024),
        cost_estimate=pl.CostEstimate(
            flops=4 * resid.size, bytes_accessed=20 * resid.size, transcendentals=0
        ),
    )(sums, curved_in, curved_out, resid, direc)


def apart(array):
    turned = with_layout_constraint(jnp.transpose(array, (1, 0, 2)), Layout((0, 1, 2)))
    return lax.optimization_barrier(turned)


def on_device(states, task_weights, pad_mask, direction, residual):
    sections = lax.axis_size("section")
    tasks = lax.axis_size("task")
    shards = lax.axis_size("fsdp")
    section_id = lax.axis_index("section")
    task_id = lax.axis_index("task")
    shard_id = lax.axis_index("fsdp")
    w_in = task_weights[0, 0, 0]
    w_out = task_weights[0, 0, 1]
    width, hidden = w_in.shape
    row_count = states.shape[1]
    joined = row_count * shards
    block = width // tasks
    piece = block // shards
    direc_local = direction[0]
    resid_local = residual[0]

    direc_apart = apart(direc_local)
    resid_apart = apart(resid_local)
    narrow = [direc_apart[i].astype(jnp.bfloat16) for i in range(2)]

    def direction_for(k):
        at = (shard_id ^ k) * hidden
        return jnp.stack([lax.dynamic_slice_in_dim(part, at, hidden, 1) for part in narrow])

    chunks = [direction_for(k) for k in range(shards)]
    pieces = [chunks[0]] + [send(chunks[k], across(k, range(sections))) for k in range(1, shards - 1)]
    pieces.append(send(chunks[-1], across(shards - 1, range(sections - 1))))

    def features_for(array):
        return lambda k: lax.dynamic_slice_in_dim(array, (task_id ^ k) * block, block, 1)

    own_inputs = [states[0]]
    packed = []
    rows_all = gather_rows(states[0], 0, 0)
    for layer in range(sections):
        normed = normalize(rows_all.astype(jnp.float32))
        normed_b = normed.astype(jnp.bfloat16)
        preact = dot(normed_b, w_in)
        acted, slope = jax.jvp(gelu_tanh, (preact,), (jnp.ones_like(preact),))
        acted_b = acted.astype(jnp.bfloat16)
        packed.append(
            task_partners(
                lambda k: jnp.concatenate([features_for(normed_b)(k), acted_b], axis=1), layer
            )
        )
        if layer + 1 < sections:
            mixed = across_hidden(acted_b, w_out)
            mixed = scatter_sum(mixed, layer, 0)
            own_rows = (own_inputs[layer].astype(jnp.float32) + mixed).astype(jnp.bfloat16)
            if layer == 0:
                own_rows, pieces[1:3] = tie(own_rows, pieces[1:3])
            own_rows, packed[layer] = tie(own_rows, packed[layer])
            own_inputs.append(own_rows)
            arrived = gather_rows(own_rows, 0, layer + 1)
            if layer == 0:
                arrived, (chunks[-1], pieces[-1]) = tie(arrived, (chunks[-1], pieces[-1]))
                late = send(chunks[-1], across(shards - 1, [sections - 1]))
                pieces[-1] = jnp.where(section_id == sections - 1, late, pieces[-1])
            rows_all = jnp.where(section_id == layer + 1, arrived, rows_all)

    steering = in_order(pieces, shard_id, 1)
    steer_in, steer_out = steering[0], steering[1]

    parts = packed[-1]
    for layer in range(sections - 1):
        here = section_id == layer
        for k in range(1, tasks):
            parts[k] = jnp.where(here, packed[layer][k], parts[k])
    normed_tasks = jnp.concatenate([part[:, :block] for part in parts], axis=0)
    acted_tasks = jnp.concatenate([part[:, block:] for part in parts], axis=0)
    steered_parts = dot(normed_tasks, steer_in).reshape(tasks, joined, hidden)
    turned_parts = across_hidden(acted_tasks, steer_out).reshape(tasks, joined, block)
    parts = task_partners(
        lambda k: jnp.concatenate(
            [
                steered_parts[k].astype(jnp.bfloat16),
                turned_parts[k].astype(jnp.bfloat16),
            ],
            axis=1,
        )
    )
    parts, resid_apart = tie(parts, resid_apart)
    steered = sum((part[:, :hidden].astype(jnp.float32) for part in parts[1:]), steered_parts[0])
    turned = in_order([part[:, hidden:] for part in parts], task_id, 1).astype(jnp.float32)

    own_dot = jnp.zeros((row_count, width), jnp.bfloat16)
    for layer in range(sections):
        if layer == 0:
            preact_dot = steered
        else:
            dots_all = gather_rows(own_dot, 0, layer)
            normed_dot = jax.jvp(
                normalize, (rows_all.astype(jnp.float32),), (dots_all.astype(jnp.float32),)
            )[1]
            preact_dot = dot(normed_dot.astype(jnp.bfloat16), w_in) + steered
        acted_dot_b = (slope * preact_dot).astype(jnp.bfloat16)
        mixed_dot = scatter_sum(across_hidden(acted_dot_b, w_out) + turned, layer, 0)
        own_dot = (own_dot.astype(jnp.float32) + mixed_dot).astype(jnp.bfloat16)

    own_bar = own_dot * pad_mask[0][:, None].astype(jnp.bfloat16)
    bars_all = jnp.zeros((joined, width), jnp.bfloat16)
    for layer in reversed(range(sections)):
        arrived = gather_rows(own_bar, 0, layer)
        bars_all = jnp.where(section_id == layer, arrived, bars_all)
        preact_bar = (dot(bars_all, w_out) * slope).astype(jnp.bfloat16)
        if layer > 0:
            normed_bar = scatter_sum(across_hidden(preact_bar, w_in), layer, 0)
            pullback = jax.vjp(normalize, own_inputs[layer].astype(jnp.float32))[1]
            own_bar = (own_bar.astype(jnp.float32) + pullback(normed_bar)[0]).astype(jnp.bfloat16)

    def to_owners(curved):
        curved = curved.astype(jnp.bfloat16).reshape(shards, piece, hidden)

        def curved_for(k):
            return lax.dynamic_index_in_dim(curved, shard_id ^ k, 0, keepdims=False)

        return in_order(fsdp_partners(curved_for), shard_id, 1)

    bars_tasks = jnp.concatenate(task_partners(features_for(bars_all)), axis=0)
    curved_out = to_owners(across_tokens(bars_tasks, acted_tasks))
    preact_bars_tasks = jnp.concatenate(task_partners(lambda k: preact_bar), axis=0)
    curved_in = to_owners(across_tokens(normed_tasks, preact_bars_tasks))
    products = [curved.astype(jnp.float32) for curved in (curved_in, curved_out)]

    def folded(values):
        blocks = [
            value[:, i * hidden : (i + 1) * hidden] for value in values for i in range(shards)
        ]
        return jnp.sum(sum(blocks), axis=0)

    sums = sum_everywhere(
        jnp.stack(
            [
                folded([resid_apart[i] * resid_apart[i] for i in range(2)]),
                folded([direc_apart[i] * products[i] for i in range(2)]),
                folded([resid_apart[i] * products[i] for i in range(2)]),
                folded([products[i] * products[i] for i in range(2)]),
            ]
        )
    )
    resid_next, direc_next, step_size = update(
        sums, curved_in, curved_out, resid_local, direc_local, hidden
    )
    return (resid_next[None], direc_next[None], step_size[0, 0])


def solution(mesh):
    placed = (
        P("task", "fsdp", None),
        P("task", "section", None, None, "fsdp"),
        P("task", "fsdp"),
        P("section", ("task", "fsdp"), None, None),
        P("section", ("task", "fsdp"), None, None),
    )
    return jax.shard_map(
        on_device,
        mesh=mesh,
        in_specs=placed,
        out_specs=(
            P("section", ("task", "fsdp"), None, None),
            P("section", ("task", "fsdp"), None, None),
            P(),
        ),
        check_vma=False,
    )
```

```python
import jax
import jax.numpy as jnp
from jax import lax
from jax.experimental import pallas as pl
from jax.experimental.pallas import tpu as pltpu
from jax.experimental.layout import Layout, with_layout_constraint
from jax.sharding import PartitionSpec as P

ALL = ("section", "task", "fsdp")
eps_norm = 1e-06


def normalize(token_rows):
    return token_rows * lax.rsqrt(
        jnp.mean(token_rows * token_rows, axis=-1, keepdims=True) + eps_norm
    )


def gelu_tanh(values):
    return jax.nn.gelu(values, approximate=True)


def across_hidden(left_side, right_side):
    return lax.dot_general(
        left_side, right_side, (((1,), (1,)), ((), ())), preferred_element_type=jnp.float32
    )


def across_tokens(left_side, right_side):
    return lax.dot_general(
        left_side, right_side, (((0,), (0,)), ((), ())), preferred_element_type=jnp.float32
    )


def dot(left_side, right_side):
    return jnp.dot(left_side, right_side, preferred_element_type=jnp.float32)


def send(value, route):
    sections, tasks, shards = (lax.axis_size(axis) for axis in ALL)
    pairs = []
    for s in range(sections):
        for t in range(tasks):
            for f in range(shards):
                target = route(s, t, f)
                if target is not None:
                    to_s, to_t, to_f = target
                    pairs.append(
                        ((s * tasks + t) * shards + f, (to_s * tasks + to_t) * shards + to_f)
                    )
    return lax.ppermute(value, ALL, pairs)


def between(start, end, k):
    return lambda s, t, f: (end, t, f ^ k) if s == start else None


def gather_rows(rows, start, end):
    parts = []
    for k in range(lax.axis_size("fsdp")):
        if k == 0 and start == end:
            parts.append(rows)
        else:
            parts.append(send(rows, between(start, end, k)))
    return jnp.concatenate(parts, axis=0)


def scatter_sum(partial, start, end):
    shards = lax.axis_size("fsdp")
    blocks = partial.reshape(shards, partial.shape[0] // shards, partial.shape[1])
    total = None
    for k in range(shards):
        if k == 0 and start == end:
            part = blocks[0]
        else:
            part = send(blocks[k].astype(jnp.bfloat16), between(start, end, k)).astype(jnp.float32)
        total = part if total is None else total + part
    return total


def task_partners(value_of, section=None):
    def route(k):
        return lambda s, t, f: (s, t ^ k, f) if section in (None, s) else None

    parts = [value_of(0)]
    for k in range(1, lax.axis_size("task")):
        parts.append(send(value_of(k), route(k)))
    return parts


def across(k, held_by):
    return lambda s, t, f: (s, t, f ^ k) if s in held_by else None


def fsdp_partners(value_of):
    parts = [value_of(0)]
    for k in range(1, lax.axis_size("fsdp")):
        parts.append(send(value_of(k), lambda s, t, f, k=k: (s, t, f ^ k)))
    return parts


def tie(value, other):
    return lax.optimization_barrier((value, other))


def in_order(parts, index, axis):
    stacked = jnp.stack(parts)
    return jnp.concatenate(
        [
            lax.dynamic_index_in_dim(stacked, index ^ j, 0, keepdims=False)
            for j in range(len(parts))
        ],
        axis=axis,
    )


def sum_everywhere(value):
    for axis in ALL:
        count = lax.axis_size(axis)
        parts = [value]
        for k in range(1, count):
            parts.append(lax.ppermute(value, axis, [(i, i ^ k) for i in range(count)]))
        while len(parts) > 1:
            parts = [parts[i] + parts[i + 1] for i in range(0, len(parts), 2)]
        value = parts[0]
    return value


def update_kernel(sums_ref, in_ref, out_ref, resid_ref, direc_ref, resid_next, direc_next, step_ref):
    start_norm, curvature, crossed, squared = (
        jnp.sum(sums_ref[i : i + 1, :], axis=1, keepdims=True) for i in range(4)
    )
    step_size = start_norm / curvature
    next_norm = start_norm - 2.0 * step_size * crossed + step_size * step_size * squared
    ratio = next_norm / start_norm
    step_ref[...] = step_size
    for i, product in ((0, in_ref), (1, out_ref)):
        fresh = resid_ref[:, i, :] - step_size * product[...].astype(jnp.float32)
        resid_next[:, i, :] = fresh
        direc_next[:, i, :] = fresh + ratio * direc_ref[:, i, :]


def update(sums, curved_in, curved_out, resid, direc, columns):
    rows, pair, total = resid.shape
    native = pl.BlockSpec((rows, pair, columns), lambda i: (0, 0, i))
    flat = pl.BlockSpec((rows, columns), lambda i: (0, i))
    return pl.pallas_call(
        update_kernel,
        grid=(total // columns,),
        in_specs=[pl.BlockSpec(sums.shape, lambda i: (0, 0)), flat, flat, native, native],
        out_specs=[native, native, pl.BlockSpec((1, 1), lambda i: (0, 0))],
        out_shape=[jax.ShapeDtypeStruct(resid.shape, jnp.float32)] * 2
        + [jax.ShapeDtypeStruct((1, 1), jnp.float32)],
        compiler_params=pltpu.CompilerParams(vmem_limit_bytes=58 * 1024 * 1024),
        cost_estimate=pl.CostEstimate(
            flops=4 * resid.size, bytes_accessed=20 * resid.size, transcendentals=0
        ),
    )(sums, curved_in, curved_out, resid, direc)


def apart(array):
    turned = with_layout_constraint(jnp.transpose(array, (1, 0, 2)), Layout((0, 1, 2)))
    return lax.optimization_barrier(turned)


def on_device(states, task_weights, pad_mask, direction, residual):
    sections = lax.axis_size("section")
    tasks = lax.axis_size("task")
    shards = lax.axis_size("fsdp")
    section_id = lax.axis_index("section")
    task_id = lax.axis_index("task")
    shard_id = lax.axis_index("fsdp")
    w_in = task_weights[0, 0, 0]
    w_out = task_weights[0, 0, 1]
    width, hidden = w_in.shape
    row_count = states.shape[1]
    joined = row_count * shards
    block = width // tasks
    piece = block // shards
    direc_local = direction[0]
    resid_local = residual[0]

    direc_apart = apart(direc_local)
    resid_apart = apart(resid_local)
    narrow = [direc_apart[i].astype(jnp.bfloat16) for i in range(2)]

    def direction_for(k):
        at = (shard_id ^ k) * hidden
        return jnp.stack([lax.dynamic_slice_in_dim(part, at, hidden, 1) for part in narrow])

    chunks = [direction_for(k) for k in range(shards)]
    pieces = [chunks[0]] + [send(chunks[k], across(k, range(sections))) for k in range(1, shards - 1)]
    pieces.append(send(chunks[-1], across(shards - 1, range(sections - 1))))

    def features_for(array):
        return lambda k: lax.dynamic_slice_in_dim(array, (task_id ^ k) * block, block, 1)

    own_inputs = [states[0]]
    packed = []
    rows_all = gather_rows(states[0], 0, 0)
    for layer in range(sections):
        normed = normalize(rows_all.astype(jnp.float32))
        normed_b = normed.astype(jnp.bfloat16)
        preact = dot(normed_b, w_in)
        acted, slope = jax.jvp(gelu_tanh, (preact,), (jnp.ones_like(preact),))
        acted_b = acted.astype(jnp.bfloat16)
        packed.append(
            task_partners(
                lambda k: jnp.concatenate([features_for(normed_b)(k), acted_b], axis=1), layer
            )
        )
        if layer + 1 < sections:
            mixed = across_hidden(acted_b, w_out)
            mixed = scatter_sum(mixed, layer, 0)
            own_rows = (own_inputs[layer].astype(jnp.float32) + mixed).astype(jnp.bfloat16)
            if layer == 0:
                own_rows, pieces[1:3] = tie(own_rows, pieces[1:3])
            own_rows, packed[layer] = tie(own_rows, packed[layer])
            own_inputs.append(own_rows)
            arrived = gather_rows(own_rows, 0, layer + 1)
            if layer == 0:
                arrived, (chunks[-1], pieces[-1]) = tie(arrived, (chunks[-1], pieces[-1]))
                late = send(chunks[-1], across(shards - 1, [sections - 1]))
                pieces[-1] = jnp.where(section_id == sections - 1, late, pieces[-1])
            rows_all = jnp.where(section_id == layer + 1, arrived, rows_all)

    steering = in_order(pieces, shard_id, 1)
    steer_in, steer_out = steering[0], steering[1]

    parts = packed[-1]
    for layer in range(sections - 1):
        here = section_id == layer
        for k in range(1, tasks):
            parts[k] = jnp.where(here, packed[layer][k], parts[k])
    normed_tasks = jnp.concatenate([part[:, :block] for part in parts], axis=0)
    acted_tasks = jnp.concatenate([part[:, block:] for part in parts], axis=0)
    steered_parts = dot(normed_tasks, steer_in).reshape(tasks, joined, hidden)
    turned_parts = across_hidden(acted_tasks, steer_out).reshape(tasks, joined, block)
    payloads = [
        jnp.concatenate([value[k].astype(jnp.bfloat16) for value in (steered_parts, turned_parts)], axis=1)
        for k in range(tasks)
    ]
    steered, turned = [], []
    for layer in range(sections):
        parts = task_partners(lambda k: payloads[k], layer)
        if layer == sections - 1:
            parts, resid_apart = tie(parts, resid_apart)
        arrived = (part[:, :hidden].astype(jnp.float32) for part in parts[1:])
        steered.append(sum(arrived, steered_parts[0]))
        arrived = in_order([part[:, hidden:] for part in parts], task_id, 1)
        turned.append(arrived.astype(jnp.float32))

    own_dot = jnp.zeros((row_count, width), jnp.bfloat16)
    for layer in range(sections):
        if layer == 0:
            preact_dot = steered[layer]
        else:
            dots_all = gather_rows(own_dot, 0, layer)
            normed_dot = jax.jvp(
                normalize, (rows_all.astype(jnp.float32),), (dots_all.astype(jnp.float32),)
            )[1]
            preact_dot = dot(normed_dot.astype(jnp.bfloat16), w_in) + steered[layer]
        acted_dot_b = (slope * preact_dot).astype(jnp.bfloat16)
        mixed_dot = scatter_sum(across_hidden(acted_dot_b, w_out) + turned[layer], layer, 0)
        own_dot = (own_dot.astype(jnp.float32) + mixed_dot).astype(jnp.bfloat16)

    own_bar = own_dot * pad_mask[0][:, None].astype(jnp.bfloat16)
    bars_all = jnp.zeros((joined, width), jnp.bfloat16)
    for layer in reversed(range(sections)):
        arrived = gather_rows(own_bar, 0, layer)
        bars_all = jnp.where(section_id == layer, arrived, bars_all)
        preact_bar = (dot(bars_all, w_out) * slope).astype(jnp.bfloat16)
        if layer > 0:
            normed_bar = scatter_sum(across_hidden(preact_bar, w_in), layer, 0)
            pullback = jax.vjp(normalize, own_inputs[layer].astype(jnp.float32))[1]
            own_bar = (own_bar.astype(jnp.float32) + pullback(normed_bar)[0]).astype(jnp.bfloat16)

    def to_owners(curved):
        curved = curved.astype(jnp.bfloat16).reshape(shards, piece, hidden)

        def curved_for(k):
            return lax.dynamic_index_in_dim(curved, shard_id ^ k, 0, keepdims=False)

        return in_order(fsdp_partners(curved_for), shard_id, 1)

    bars_tasks = jnp.concatenate(task_partners(features_for(bars_all)), axis=0)
    curved_out = to_owners(across_tokens(bars_tasks, acted_tasks))
    preact_bars_tasks = jnp.concatenate(task_partners(lambda k: preact_bar), axis=0)
    curved_in = to_owners(across_tokens(normed_tasks, preact_bars_tasks))
    products = [curved.astype(jnp.float32) for curved in (curved_in, curved_out)]

    def folded(values):
        blocks = [
            value[:, i * hidden : (i + 1) * hidden] for value in values for i in range(shards)
        ]
        return jnp.sum(sum(blocks), axis=0)

    sums = sum_everywhere(
        jnp.stack(
            [
                folded([resid_apart[i] * resid_apart[i] for i in range(2)]),
                folded([direc_apart[i] * products[i] for i in range(2)]),
                folded([resid_apart[i] * products[i] for i in range(2)]),
                folded([products[i] * products[i] for i in range(2)]),
            ]
        )
    )
    resid_next, direc_next, step_size = update(
        sums, curved_in, curved_out, resid_local, direc_local, hidden
    )
    return (resid_next[None], direc_next[None], step_size[0, 0])


def solution(mesh):
    placed = (
        P("task", "fsdp", None),
        P("task", "section", None, None, "fsdp"),
        P("task", "fsdp"),
        P("section", ("task", "fsdp"), None, None),
        P("section", ("task", "fsdp"), None, None),
    )
    return jax.shard_map(
        on_device,
        mesh=mesh,
        in_specs=placed,
        out_specs=(
            P("section", ("task", "fsdp"), None, None),
            P("section", ("task", "fsdp"), None, None),
            P(),
        ),
        check_vma=False,
    )
```

```python
import jax
import jax.numpy as jnp
from jax import lax
from jax.experimental import pallas as pl
from jax.experimental.pallas import tpu as pltpu
from jax.experimental.layout import Layout, with_layout_constraint
from jax.sharding import PartitionSpec as P

ALL = ("section", "task", "fsdp")
eps_norm = 1e-06


def normalize(token_rows):
    return token_rows * lax.rsqrt(
        jnp.mean(token_rows * token_rows, axis=-1, keepdims=True) + eps_norm
    )


def gelu_tanh(values):
    return jax.nn.gelu(values, approximate=True)


def across_hidden(left_side, right_side):
    return lax.dot_general(
        left_side, right_side, (((1,), (1,)), ((), ())), preferred_element_type=jnp.float32
    )


def across_tokens(left_side, right_side):
    return lax.dot_general(
        left_side, right_side, (((0,), (0,)), ((), ())), preferred_element_type=jnp.float32
    )


def dot(left_side, right_side):
    return jnp.dot(left_side, right_side, preferred_element_type=jnp.float32)


def send(value, route):
    sections, tasks, shards = (lax.axis_size(axis) for axis in ALL)
    pairs = []
    for s in range(sections):
        for t in range(tasks):
            for f in range(shards):
                target = route(s, t, f)
                if target is not None:
                    to_s, to_t, to_f = target
                    pairs.append(
                        ((s * tasks + t) * shards + f, (to_s * tasks + to_t) * shards + to_f)
                    )
    return lax.ppermute(value, ALL, pairs)


def between(start, end, k):
    return lambda s, t, f: (end, t, f ^ k) if s == start else None


def gather_rows(rows, start, end):
    parts = []
    for k in range(lax.axis_size("fsdp")):
        if k == 0 and start == end:
            parts.append(rows)
        else:
            parts.append(send(rows, between(start, end, k)))
    return jnp.concatenate(parts, axis=0)


def scatter_sum(partial, start, end):
    shards = lax.axis_size("fsdp")
    blocks = partial.reshape(shards, partial.shape[0] // shards, partial.shape[1])
    total = None
    for k in range(shards):
        if k == 0 and start == end:
            part = blocks[0]
        else:
            part = send(blocks[k].astype(jnp.bfloat16), between(start, end, k)).astype(jnp.float32)
        total = part if total is None else total + part
    return total


def task_partners(value_of, section=None):
    def route(k):
        return lambda s, t, f: (s, t ^ k, f) if section in (None, s) else None

    parts = [value_of(0)]
    for k in range(1, lax.axis_size("task")):
        parts.append(send(value_of(k), route(k)))
    return parts


def across(k, held_by):
    return lambda s, t, f: (s, t, f ^ k) if s in held_by else None


def fsdp_partners(value_of):
    parts = [value_of(0)]
    for k in range(1, lax.axis_size("fsdp")):
        parts.append(send(value_of(k), lambda s, t, f, k=k: (s, t, f ^ k)))
    return parts


def tie(value, other):
    return lax.optimization_barrier((value, other))


def in_order(parts, index, axis):
    stacked = jnp.stack(parts)
    return jnp.concatenate(
        [
            lax.dynamic_index_in_dim(stacked, index ^ j, 0, keepdims=False)
            for j in range(len(parts))
        ],
        axis=axis,
    )


def sum_everywhere(value):
    for axis in ALL:
        count = lax.axis_size(axis)
        parts = [value]
        for k in range(1, count):
            parts.append(lax.ppermute(value, axis, [(i, i ^ k) for i in range(count)]))
        while len(parts) > 1:
            parts = [parts[i] + parts[i + 1] for i in range(0, len(parts), 2)]
        value = parts[0]
    return value


def update_kernel(sums_ref, in_ref, out_ref, resid_ref, direc_ref, resid_next, direc_next, step_ref):
    start_norm, curvature, crossed, squared = (
        jnp.sum(sums_ref[i : i + 1, :], axis=1, keepdims=True) for i in range(4)
    )
    step_size = start_norm / curvature
    next_norm = start_norm - 2.0 * step_size * crossed + step_size * step_size * squared
    ratio = next_norm / start_norm
    step_ref[...] = step_size
    for i, product in ((0, in_ref), (1, out_ref)):
        fresh = resid_ref[:, i, :] - step_size * product[...].astype(jnp.float32)
        resid_next[:, i, :] = fresh
        direc_next[:, i, :] = fresh + ratio * direc_ref[:, i, :]


def update(sums, curved_in, curved_out, resid, direc, columns):
    rows, pair, total = resid.shape
    native = pl.BlockSpec((rows, pair, columns), lambda i: (0, 0, i))
    flat = pl.BlockSpec((rows, columns), lambda i: (0, i))
    return pl.pallas_call(
        update_kernel,
        grid=(total // columns,),
        in_specs=[pl.BlockSpec(sums.shape, lambda i: (0, 0)), flat, flat, native, native],
        out_specs=[native, native, pl.BlockSpec((1, 1), lambda i: (0, 0))],
        out_shape=[jax.ShapeDtypeStruct(resid.shape, jnp.float32)] * 2
        + [jax.ShapeDtypeStruct((1, 1), jnp.float32)],
        compiler_params=pltpu.CompilerParams(vmem_limit_bytes=40 * 1024 * 1024),
        cost_estimate=pl.CostEstimate(
            flops=4 * resid.size, bytes_accessed=20 * resid.size, transcendentals=0
        ),
    )(sums, curved_in, curved_out, resid, direc)


def apart(array):
    turned = with_layout_constraint(jnp.transpose(array, (1, 0, 2)), Layout((0, 1, 2)))
    return lax.optimization_barrier(turned)


def on_device(states, task_weights, pad_mask, direction, residual):
    sections = lax.axis_size("section")
    tasks = lax.axis_size("task")
    shards = lax.axis_size("fsdp")
    section_id = lax.axis_index("section")
    task_id = lax.axis_index("task")
    shard_id = lax.axis_index("fsdp")
    w_in = task_weights[0, 0, 0]
    w_out = task_weights[0, 0, 1]
    width, hidden = w_in.shape
    row_count = states.shape[1]
    joined = row_count * shards
    block = width // tasks
    piece = block // shards
    direc_local = direction[0]
    resid_local = residual[0]

    direc_apart = apart(direc_local)
    resid_apart = apart(resid_local)
    narrow = [direc_apart[i].astype(jnp.bfloat16) for i in range(2)]

    def direction_for(k):
        at = (shard_id ^ k) * hidden
        return jnp.stack([lax.dynamic_slice_in_dim(part, at, hidden, 1) for part in narrow])

    chunks = [direction_for(k) for k in range(shards)]
    pieces = [chunks[0]] + [send(chunks[k], across(k, range(sections))) for k in range(1, shards - 1)]
    pieces.append(send(chunks[-1], across(shards - 1, range(sections - 1))))

    def features_for(array):
        return lambda k: lax.dynamic_slice_in_dim(array, (task_id ^ k) * block, block, 1)

    own_inputs = [states[0]]
    packed = []
    rows_all = gather_rows(states[0], 0, 0)
    for layer in range(sections):
        normed = normalize(rows_all.astype(jnp.float32))
        normed_b = normed.astype(jnp.bfloat16)
        preact = dot(normed_b, w_in)
        acted, slope = jax.jvp(gelu_tanh, (preact,), (jnp.ones_like(preact),))
        acted_b = acted.astype(jnp.bfloat16)
        packed.append(
            task_partners(
                lambda k: jnp.concatenate([features_for(normed_b)(k), acted_b], axis=1), layer
            )
        )
        if layer + 1 < sections:
            mixed = across_hidden(acted_b, w_out)
            mixed = scatter_sum(mixed, layer, 0)
            own_rows = (own_inputs[layer].astype(jnp.float32) + mixed).astype(jnp.bfloat16)
            if layer == 0:
                own_rows, pieces[1:3] = tie(own_rows, pieces[1:3])
            own_rows, packed[layer] = tie(own_rows, packed[layer])
            own_inputs.append(own_rows)
            arrived = gather_rows(own_rows, 0, layer + 1)
            if layer == 0:
                arrived, (chunks[-1], pieces[-1]) = tie(arrived, (chunks[-1], pieces[-1]))
                late = send(chunks[-1], across(shards - 1, [sections - 1]))
                pieces[-1] = jnp.where(section_id == sections - 1, late, pieces[-1])
            rows_all = jnp.where(section_id == layer + 1, arrived, rows_all)

    steering = in_order(pieces, shard_id, 1)
    steer_in, steer_out = steering[0], steering[1]

    parts = packed[-1]
    for layer in range(sections - 1):
        here = section_id == layer
        for k in range(1, tasks):
            parts[k] = jnp.where(here, packed[layer][k], parts[k])
    normed_tasks = jnp.concatenate([part[:, :block] for part in parts], axis=0)
    acted_tasks = jnp.concatenate([part[:, block:] for part in parts], axis=0)
    steered_parts = dot(normed_tasks, steer_in).reshape(tasks, joined, hidden)
    turned_parts = across_hidden(acted_tasks, steer_out).reshape(tasks, joined, block)
    payloads = [
        jnp.concatenate([value[k].astype(jnp.bfloat16) for value in (steered_parts, turned_parts)], axis=1)
        for k in range(tasks)
    ]
    steered, turned = [], []
    for layer in range(sections):
        parts = task_partners(lambda k: payloads[k], layer)
        if layer == sections - 1:
            parts, resid_apart = tie(parts, resid_apart)
        arrived = (part[:, :hidden].astype(jnp.float32) for part in parts[1:])
        steered.append(sum(arrived, steered_parts[0]))
        arrived = in_order([part[:, hidden:] for part in parts], task_id, 1)
        turned.append(arrived.astype(jnp.float32))

    own_dot = jnp.zeros((row_count, width), jnp.bfloat16)
    for layer in range(sections):
        if layer == 0:
            preact_dot = steered[layer]
        else:
            dots_all = gather_rows(own_dot, 0, layer)
            normed_dot = jax.jvp(
                normalize, (rows_all.astype(jnp.float32),), (dots_all.astype(jnp.float32),)
            )[1]
            preact_dot = dot(normed_dot.astype(jnp.bfloat16), w_in) + steered[layer]
        acted_dot_b = (slope * preact_dot).astype(jnp.bfloat16)
        mixed_dot = scatter_sum(across_hidden(acted_dot_b, w_out) + turned[layer], layer, 0)
        own_dot = (own_dot.astype(jnp.float32) + mixed_dot).astype(jnp.bfloat16)

    own_bar = own_dot * pad_mask[0][:, None].astype(jnp.bfloat16)
    bars_all = jnp.zeros((joined, width), jnp.bfloat16)
    for layer in reversed(range(sections)):
        arrived = gather_rows(own_bar, 0, layer)
        bars_all = jnp.where(section_id == layer, arrived, bars_all)
        preact_bar = (dot(bars_all, w_out) * slope).astype(jnp.bfloat16)
        if layer > 0:
            normed_bar = scatter_sum(across_hidden(preact_bar, w_in), layer, 0)
            pullback = jax.vjp(normalize, own_inputs[layer].astype(jnp.float32))[1]
            own_bar = (own_bar.astype(jnp.float32) + pullback(normed_bar)[0]).astype(jnp.bfloat16)

    def to_owners(curved):
        curved = curved.astype(jnp.bfloat16).reshape(shards, piece, hidden)

        def curved_for(k):
            return lax.dynamic_index_in_dim(curved, shard_id ^ k, 0, keepdims=False)

        return in_order(fsdp_partners(curved_for), shard_id, 1)

    bars_tasks = jnp.concatenate(task_partners(features_for(bars_all)), axis=0)
    curved_out = to_owners(across_tokens(bars_tasks, acted_tasks))
    preact_bars_tasks = jnp.concatenate(task_partners(lambda k: preact_bar), axis=0)
    curved_in = to_owners(across_tokens(normed_tasks, preact_bars_tasks))
    products = [curved.astype(jnp.float32) for curved in (curved_in, curved_out)]

    def folded(values):
        blocks = [
            value[:, i * hidden : (i + 1) * hidden] for value in values for i in range(shards)
        ]
        return jnp.sum(sum(blocks), axis=0)

    sums = sum_everywhere(
        jnp.stack(
            [
                folded([resid_apart[i] * resid_apart[i] for i in range(2)]),
                folded([direc_apart[i] * products[i] for i in range(2)]),
                folded([resid_apart[i] * products[i] for i in range(2)]),
                folded([products[i] * products[i] for i in range(2)]),
            ]
        )
    )
    resid_next, direc_next, step_size = update(
        sums, curved_in, curved_out, resid_local, direc_local, hidden
    )
    return (resid_next[None], direc_next[None], step_size[0, 0])


def solution(mesh):
    placed = (
        P("task", "fsdp", None),
        P("task", "section", None, None, "fsdp"),
        P("task", "fsdp"),
        P("section", ("task", "fsdp"), None, None),
        P("section", ("task", "fsdp"), None, None),
    )
    return jax.shard_map(
        on_device,
        mesh=mesh,
        in_specs=placed,
        out_specs=(
            P("section", ("task", "fsdp"), None, None),
            P("section", ("task", "fsdp"), None, None),
            P(),
        ),
        check_vma=False,
    )
```

```python
import jax
import jax.numpy as jnp
from jax import lax
from jax.experimental import pallas as pl
from jax.experimental.pallas import tpu as pltpu
from jax.experimental.layout import Layout, with_layout_constraint
from jax.sharding import PartitionSpec as P

ALL = ("section", "task", "fsdp")
eps_norm = 1e-06


def normalize(token_rows):
    return token_rows * lax.rsqrt(
        jnp.mean(token_rows * token_rows, axis=-1, keepdims=True) + eps_norm
    )


def gelu_tanh(values):
    return jax.nn.gelu(values, approximate=True)


def across_hidden(left_side, right_side):
    return lax.dot_general(
        left_side, right_side, (((1,), (1,)), ((), ())), preferred_element_type=jnp.float32
    )


def across_tokens(left_side, right_side):
    return lax.dot_general(
        left_side, right_side, (((0,), (0,)), ((), ())), preferred_element_type=jnp.float32
    )


def dot(left_side, right_side):
    return jnp.dot(left_side, right_side, preferred_element_type=jnp.float32)


def send(value, route):
    sections, tasks, shards = (lax.axis_size(axis) for axis in ALL)
    pairs = []
    for s in range(sections):
        for t in range(tasks):
            for f in range(shards):
                target = route(s, t, f)
                if target is not None:
                    to_s, to_t, to_f = target
                    pairs.append(
                        ((s * tasks + t) * shards + f, (to_s * tasks + to_t) * shards + to_f)
                    )
    return lax.ppermute(value, ALL, pairs)


def between(start, end, k):
    return lambda s, t, f: (end, t, f ^ k) if s == start else None


def gather_rows(rows, start, end):
    parts = []
    for k in range(lax.axis_size("fsdp")):
        if k == 0 and start == end:
            parts.append(rows)
        else:
            parts.append(send(rows, between(start, end, k)))
    return jnp.concatenate(parts, axis=0)


def scatter_sum(partial, start, end):
    shards = lax.axis_size("fsdp")
    blocks = partial.reshape(shards, partial.shape[0] // shards, partial.shape[1])
    total = None
    for k in range(shards):
        if k == 0 and start == end:
            part = blocks[0]
        else:
            part = send(blocks[k].astype(jnp.bfloat16), between(start, end, k)).astype(jnp.float32)
        total = part if total is None else total + part
    return total


def task_partners(value_of, section=None):
    def route(k):
        return lambda s, t, f: (s, t ^ k, f) if section in (None, s) else None

    parts = [value_of(0)]
    for k in range(1, lax.axis_size("task")):
        parts.append(send(value_of(k), route(k)))
    return parts


def across(k, held_by):
    return lambda s, t, f: (s, t, f ^ k) if s in held_by else None


def fsdp_partners(value_of):
    parts = [value_of(0)]
    for k in range(1, lax.axis_size("fsdp")):
        parts.append(send(value_of(k), lambda s, t, f, k=k: (s, t, f ^ k)))
    return parts


def tie(value, other):
    return lax.optimization_barrier((value, other))


def in_order(parts, index, axis):
    stacked = jnp.stack(parts)
    return jnp.concatenate(
        [
            lax.dynamic_index_in_dim(stacked, index ^ j, 0, keepdims=False)
            for j in range(len(parts))
        ],
        axis=axis,
    )


def sum_everywhere(value):
    for axis in ALL:
        count = lax.axis_size(axis)
        parts = [value]
        for k in range(1, count):
            parts.append(lax.ppermute(value, axis, [(i, i ^ k) for i in range(count)]))
        while len(parts) > 1:
            parts = [parts[i] + parts[i + 1] for i in range(0, len(parts), 2)]
        value = parts[0]
    return value


def update_kernel(sums_ref, in_ref, out_ref, resid_ref, direc_ref, resid_next, direc_next, step_ref):
    start_norm, curvature, crossed, squared = (
        jnp.sum(sums_ref[i : i + 1, :], axis=1, keepdims=True) for i in range(4)
    )
    step_size = start_norm / curvature
    next_norm = start_norm - 2.0 * step_size * crossed + step_size * step_size * squared
    ratio = next_norm / start_norm
    step_ref[...] = step_size
    for i, product in ((0, in_ref), (1, out_ref)):
        fresh = resid_ref[:, i, :] - step_size * product[...].astype(jnp.float32)
        resid_next[:, i, :] = fresh
        direc_next[:, i, :] = fresh + ratio * direc_ref[:, i, :]


def update(sums, curved_in, curved_out, resid, direc, columns):
    rows, pair, total = resid.shape
    native = pl.BlockSpec((rows, pair, columns), lambda i: (0, 0, i))
    flat = pl.BlockSpec((rows, columns), lambda i: (0, i))
    return pl.pallas_call(
        update_kernel,
        grid=(total // columns,),
        in_specs=[pl.BlockSpec(sums.shape, lambda i: (0, 0)), flat, flat, native, native],
        out_specs=[native, native, pl.BlockSpec((1, 1), lambda i: (0, 0))],
        out_shape=[jax.ShapeDtypeStruct(resid.shape, jnp.float32)] * 2
        + [jax.ShapeDtypeStruct((1, 1), jnp.float32)],
        compiler_params=pltpu.CompilerParams(vmem_limit_bytes=40 * 1024 * 1024),
        cost_estimate=pl.CostEstimate(
            flops=4 * resid.size, bytes_accessed=20 * resid.size, transcendentals=0
        ),
    )(sums, curved_in, curved_out, resid, direc)


def apart(array):
    turned = with_layout_constraint(jnp.transpose(array, (1, 0, 2)), Layout((0, 1, 2)))
    return lax.optimization_barrier(turned)


def on_device(states, task_weights, pad_mask, direction, residual):
    sections = lax.axis_size("section")
    tasks = lax.axis_size("task")
    shards = lax.axis_size("fsdp")
    section_id = lax.axis_index("section")
    task_id = lax.axis_index("task")
    shard_id = lax.axis_index("fsdp")
    w_in = task_weights[0, 0, 0]
    w_out = task_weights[0, 0, 1]
    width, hidden = w_in.shape
    row_count = states.shape[1]
    joined = row_count * shards
    block = width // tasks
    piece = block // shards
    direc_local = direction[0]
    resid_local = residual[0]

    direc_apart = apart(direc_local)
    resid_apart = apart(resid_local)
    narrow = [direc_apart[i].astype(jnp.bfloat16) for i in range(2)]

    def direction_for(k):
        at = (shard_id ^ k) * hidden
        return jnp.stack([lax.dynamic_slice_in_dim(part, at, hidden, 1) for part in narrow])

    chunks = [direction_for(k) for k in range(shards)]
    pieces = [chunks[0]] + [send(chunks[k], across(k, range(sections))) for k in range(1, shards - 1)]
    pieces.append(send(chunks[-1], across(shards - 1, range(sections - 1))))

    def features_for(array):
        return lambda k: lax.dynamic_slice_in_dim(array, (task_id ^ k) * block, block, 1)

    own_inputs = [states[0]]
    packed = []
    rows_all = gather_rows(states[0], 0, 0)
    for layer in range(sections):
        normed = normalize(rows_all.astype(jnp.float32))
        normed_b = normed.astype(jnp.bfloat16)
        preact = dot(normed_b, w_in)
        acted, slope = jax.jvp(gelu_tanh, (preact,), (jnp.ones_like(preact),))
        acted_b = acted.astype(jnp.bfloat16)
        packed.append(
            task_partners(
                lambda k: jnp.concatenate([features_for(normed_b)(k), acted_b], axis=1), layer
            )
        )
        if layer + 1 < sections:
            mixed = across_hidden(acted_b, w_out)
            mixed = scatter_sum(mixed, layer, 0)
            own_rows = (own_inputs[layer].astype(jnp.float32) + mixed).astype(jnp.bfloat16)
            if layer == 0:
                own_rows, pieces[1:3] = tie(own_rows, pieces[1:3])
            own_rows, packed[layer] = tie(own_rows, packed[layer])
            own_inputs.append(own_rows)
            arrived = gather_rows(own_rows, 0, layer + 1)
            if layer == 0:
                arrived, (chunks[-1], pieces[-1]) = tie(arrived, (chunks[-1], pieces[-1]))
                late = send(chunks[-1], across(shards - 1, [sections - 1]))
                pieces[-1] = jnp.where(section_id == sections - 1, late, pieces[-1])
            rows_all = jnp.where(section_id == layer + 1, arrived, rows_all)

    steering = in_order(pieces, shard_id, 1)
    steer_in, steer_out = steering[0], steering[1]

    parts = packed[-1]
    for layer in range(sections - 1):
        here = section_id == layer
        for k in range(1, tasks):
            parts[k] = jnp.where(here, packed[layer][k], parts[k])
    normed_tasks = jnp.concatenate([part[:, :block] for part in parts], axis=0)
    acted_tasks = jnp.concatenate([part[:, block:] for part in parts], axis=0)
    steered_parts = dot(normed_tasks, steer_in).reshape(tasks, joined, hidden)
    turned_parts = across_hidden(acted_tasks, steer_out).reshape(tasks, joined, block)
    parts = task_partners(
        lambda k: jnp.concatenate(
            [
                steered_parts[k].astype(jnp.bfloat16),
                turned_parts[k].astype(jnp.bfloat16),
            ],
            axis=1,
        )
    )
    parts, resid_apart = tie(parts, resid_apart)
    steered = sum((part[:, :hidden].astype(jnp.float32) for part in parts[1:]), steered_parts[0])
    turned = in_order([part[:, hidden:] for part in parts], task_id, 1).astype(jnp.float32)

    own_dot = jnp.zeros((row_count, width), jnp.bfloat16)
    for layer in range(sections):
        if layer == 0:
            preact_dot = steered
        else:
            dots_all = gather_rows(own_dot, 0, layer)
            normed_dot = jax.jvp(
                normalize, (rows_all.astype(jnp.float32),), (dots_all.astype(jnp.float32),)
            )[1]
            preact_dot = dot(normed_dot.astype(jnp.bfloat16), w_in) + steered
        acted_dot_b = (slope * preact_dot).astype(jnp.bfloat16)
        mixed_dot = scatter_sum(across_hidden(acted_dot_b, w_out) + turned, layer, 0)
        own_dot = (own_dot.astype(jnp.float32) + mixed_dot).astype(jnp.bfloat16)

    own_bar = own_dot * pad_mask[0][:, None].astype(jnp.bfloat16)
    bars_all = jnp.zeros((joined, width), jnp.bfloat16)
    for layer in reversed(range(sections)):
        arrived = gather_rows(own_bar, 0, layer)
        bars_all = jnp.where(section_id == layer, arrived, bars_all)
        preact_bar = (dot(bars_all, w_out) * slope).astype(jnp.bfloat16)
        if layer > 0:
            normed_bar = scatter_sum(across_hidden(preact_bar, w_in), layer, 0)
            pullback = jax.vjp(normalize, own_inputs[layer].astype(jnp.float32))[1]
            own_bar = (own_bar.astype(jnp.float32) + pullback(normed_bar)[0]).astype(jnp.bfloat16)

    def to_owners(curved):
        curved = curved.astype(jnp.bfloat16).reshape(shards, piece, hidden)

        def curved_for(k):
            return lax.dynamic_index_in_dim(curved, shard_id ^ k, 0, keepdims=False)

        return in_order(fsdp_partners(curved_for), shard_id, 1)

    bars_tasks = jnp.concatenate(task_partners(features_for(bars_all)), axis=0)
    curved_out = to_owners(across_tokens(bars_tasks, acted_tasks))
    preact_bars_tasks = jnp.concatenate(task_partners(lambda k: preact_bar), axis=0)
    curved_in = to_owners(across_tokens(normed_tasks, preact_bars_tasks))
    products = [curved.astype(jnp.float32) for curved in (curved_in, curved_out)]

    def folded(values):
        blocks = [
            value[:, i * hidden : (i + 1) * hidden] for value in values for i in range(shards)
        ]
        return jnp.sum(sum(blocks), axis=0)

    sums = sum_everywhere(
        jnp.stack(
            [
                folded([resid_apart[i] * resid_apart[i] for i in range(2)]),
                folded([direc_apart[i] * products[i] for i in range(2)]),
                folded([resid_apart[i] * products[i] for i in range(2)]),
                folded([products[i] * products[i] for i in range(2)]),
            ]
        )
    )
    resid_next, direc_next, step_size = update(
        sums, curved_in, curved_out, resid_local, direc_local, hidden
    )
    return (resid_next[None], direc_next[None], step_size[0, 0])


def solution(mesh):
    placed = (
        P("task", "fsdp", None),
        P("task", "section", None, None, "fsdp"),
        P("task", "fsdp"),
        P("section", ("task", "fsdp"), None, None),
        P("section", ("task", "fsdp"), None, None),
    )
    return jax.shard_map(
        on_device,
        mesh=mesh,
        in_specs=placed,
        out_specs=(
            P("section", ("task", "fsdp"), None, None),
            P("section", ("task", "fsdp"), None, None),
            P(),
        ),
        check_vma=False,
    )
```
